512 devices in a mesh: replica: 4 (over z_lo, core), dp: 4 (over x), mp: 32 (over y, z_hi).
Axes of the slice: x: 4, y: 8, z: 8 (z_hi: 4, z_lo: 2; z = z_hi * 2 + z_lo), core: 2. Of those that a mesh axis runs over, the one named last changes fastest.
Arguments:
- tokens: bfloat16 [2048, 6144], P(('replica', 'dp'), 'mp'), may hold values from -6 to 6
- norm_gain: bfloat16 [6144], replicated, may hold values from 0.5 to 1.5
- joined_weight: bfloat16 [6144, 21504], P('dp', 'mp'), may hold values from -0.15625 to 0.15625
- output_grad: bfloat16 [2048, 21504], P(('replica', 'dp'), 'mp'), may hold values from -1.5 to 1.5
Outputs:
- activated: bfloat16 [2048, 21504], P(('replica', 'dp'), 'mp')
- normed_grad: bfloat16 [2048, 6144], P(('replica', 'dp'), 'mp')
- weight_grad: bfloat16 [6144, 21504], P('dp', 'mp')
The draws below stay inside these ranges and needn't reach their ends.
All inputs are finite; a program needn't handle non-finite values.
Results may differ from the reference program's by a relative error of at most 0.02.
Values may be sent and summed in bfloat16 or wider, within the bound.
A program may use at most 64 MiB of HBM per device.

```python
import jax
import jax.numpy as jnp
from jax import lax

D = 6144
TOK_DEV = 128
QKV_DEV = 288
COLS_DEV = 672
COLUMNS = 21504
TOKENS = 2048
N_REPLICA = 4
N_DP = 4
N_MP = 32


def raised(entries, stream_key, source, target, blocks, factor):
    owner, partner = [(jnp.arange(entries.shape[dim]) // (entries.shape[dim] // blocks)).reshape([-1 if axis == dim else 1 for axis in range(entries.ndim)]) for dim in (source, target)]
    chosen = jax.random.permutation(stream_key, blocks)[partner]
    strong = (owner == chosen) | (owner == (partner + blocks // 2) % blocks)
    return jnp.where(strong, factor * entries, entries)


def steps_of(key, extent, pieces, low, top_value):
    factor_of = 1.0
    for dim, blocks in pieces:
        draws = jax.random.uniform(jax.random.fold_in(jax.random.fold_in(key, 6), dim), (blocks,), jnp.float32, low / len(pieces), top_value / len(pieces))
        factor_of = factor_of * jnp.repeat(jnp.exp(draws), extent[dim] // blocks).reshape((-1,) + (1,) * (len(extent) - 1 - dim))
    return factor_of


def bell_draw(rng, dims, scale, reach, split=(), held_as=jnp.bfloat16):
    entries = jax.random.normal(rng, dims, jnp.float32) * scale
    if len(split) > 0:
        entries = steps_of(rng, dims, split, -0.22, 0.18) * entries
    return jnp.clip(entries, min=-reach, max=reach).astype(held_as)


def bell_draw_with(own_key, extent, deviation, reach, shards, heavy, kind=jnp.bfloat16):
    entries = deviation * jax.random.normal(own_key, extent, jnp.float32)
    if shards:
        entries = entries * steps_of(own_key, extent, shards, -0.22, 0.18)
    return jnp.clip(raised(entries, jax.random.fold_in(own_key, 3), *heavy), -reach, reach).astype(kind)


def setup_inputs(seed: int = 0) -> dict:
    key_list = jax.random.split(jax.random.key(seed), 5)
    return {
        "tokens": bell_draw(key_list[0], (TOKENS, D), 1.0, 6.0, ((0, 16), (1, 32))),
        "norm_gain": jnp.clip(jax.random.uniform(key_list[1], (D,), jnp.float32, 0.5, 1.5), 0.5, 1.5).astype(jnp.bfloat16),
        "joined_weight": bell_draw_with(key_list[2], (D, COLUMNS), D ** -0.5, 0.15625, ((0, 4), (1, 32)), (1, 0, 32, 2.75)),
        "output_grad": bell_draw(key_list[3], (TOKENS, COLUMNS), 0.25, 1.5, ((0, 16), (1, 32))),
    }


contract_rows = (((0,), (0,)), ((), ()))
contract_cols = (((1,), (1,)), ((), ()))

def normalize(inputs, scaling):
    values = inputs.astype(jnp.float32)
    center = lax.optimization_barrier(jnp.mean(values, axis=1, keepdims=True))
    spread = lax.optimization_barrier(jnp.mean(jnp.square(values - center), axis=1, keepdims=True))
    return ((values - center) * lax.rsqrt(spread + 1e-06) * scaling.astype(jnp.float32)).astype(jnp.bfloat16)

def reference(tokens, norm_gain, joined_weight, output_grad):
    normed = normalize(tokens, norm_gain)
    projected = jnp.dot(normed, joined_weight, preferred_element_type=jnp.float32)
    position = lax.broadcasted_iota(jnp.int32, (1, COLUMNS), 1) % COLS_DEV
    linear = position < QKV_DEV
    normal_cdf = 0.5 * (1.0 + jax.scipy.special.erf(projected * 0.7071067811865476))
    density = jnp.exp(-0.5 * projected * projected) * 0.3989422804014327
    activated = jnp.where(linear, projected, projected * normal_cdf).astype(jnp.bfloat16)
    slopes = jnp.where(linear, jnp.ones_like(projected), normal_cdf + projected * density)
    inner_grad = (output_grad.astype(jnp.float32) * slopes).astype(jnp.bfloat16)

    def column_block(running, block_index):
        offset = block_index * COLS_DEV
        grad_block = lax.dynamic_slice_in_dim(inner_grad, offset, COLS_DEV, 1)
        weight_block = lax.dynamic_slice_in_dim(joined_weight, offset, COLS_DEV, 1)
        product = lax.dot_general(grad_block, weight_block, contract_cols, preferred_element_type=jnp.float32)
        product = lax.optimization_barrier(product.astype(jnp.bfloat16))
        return (running + product.astype(jnp.float32), None)
    token_sum, _ = lax.scan(column_block, jnp.zeros((TOKENS, D), jnp.float32), jnp.arange(N_MP, dtype=jnp.int32))
    normed_grad = token_sum.astype(jnp.bfloat16)
    group_size = TOK_DEV * N_DP

    def token_block(running, block_index):
        offset = block_index * group_size
        token_rows = lax.dynamic_slice_in_dim(normed, offset, group_size, 0)
        grad_rows = lax.dynamic_slice_in_dim(inner_grad, offset, group_size, 0)
        product = lax.dot_general(token_rows, grad_rows, contract_rows, preferred_element_type=jnp.float32)
        product = lax.optimization_barrier(product.astype(jnp.bfloat16))
        return (running + product.astype(jnp.float32), None)
    weight_sum, _ = lax.scan(token_block, jnp.zeros((D, COLUMNS), jnp.float32), jnp.arange(N_REPLICA, dtype=jnp.int32))
    weight_grad = (weight_sum / N_REPLICA).astype(jnp.bfloat16)
    return (activated, normed_grad, weight_grad)
```

```python
import functools

import jax
import jax.numpy as jnp
from jax import lax
from jax.experimental import pallas as pl
from jax.experimental.pallas import tpu as pltpu
from jax.sharding import PartitionSpec as P

MESH = pl.DeviceIdType.MESH
F32 = jnp.float32
BF16 = jnp.bfloat16

NX = 4
NY = 8
NZ = 4
TOK = 128
FEAT = 192
HALF = NZ * FEAT
COLS = 672
QKV = 288
D = 6144
CHUNK = 256
SUB = TOK // 2

SEGMENTS = tuple((z * 128, z * FEAT, 128) for z in range(NZ)) + tuple(
    (512 + z * 64, z * FEAT + 128, 64) for z in range(NZ)
)


def remote(src, dst, send_sem, recv_sem, **device):
    return pltpu.make_async_remote_copy(
        src_ref=src,
        dst_ref=dst,
        send_sem=send_sem,
        recv_sem=recv_sem,
        device_id=device,
        device_id_type=MESH,
    )


def lanes_below_64(rows):
    return lax.broadcasted_iota(jnp.int32, (rows, 128), 1) < 64


def merge_stats(stack, features):
    count = stack.shape[0]
    means = stack[:, 0:1, :]
    mean = jnp.sum(means, axis=0) / count
    squares = jnp.sum(stack[:, 1:2, :], axis=0) + features * jnp.sum(
        jnp.square(means - mean[None]), axis=0
    )
    row = lax.broadcasted_iota(jnp.int32, (8, 128), 0)
    return jnp.where(row == 0, mean, jnp.where(row == 1, squares, 0.0))


def split_piece(total, z):
    tail = total[:, 512 + (z // 2) * 128 : 640 + (z // 2) * 128]
    low = lanes_below_64(SUB)
    if z % 2 == 0:
        packed = jnp.where(low, tail[:SUB], pltpu.roll(tail[SUB:], 64, 1))
    else:
        packed = jnp.where(low, pltpu.roll(tail[:SUB], 64, 1), tail[SUB:])
    return total[:, z * 128 : (z + 1) * 128], packed


def kernel(
    tok_ref, gain_ref, og_ref, w_hbm, act_ref, ng_ref, wg_hbm,
    w, stat_tx, stat_z, stat_y, stat_z_tx, block, gathered, rows, rows_t,
    proj_tx, proj_rx, proj_own, inner, part, ytx, yrx, ztx, zrx, last_tx, last_rx,
    core_tx, core_rx, lo_tx, lo_rx, done,
    w_sem, out_sem, stat_send, stat_recv, perm_send, perm_recv, zg_send, zg_recv,
    yg_send, yg_recv, px_send, px_recv, ix_send, ix_recv, ys_send, ys_recv,
    zs_send, zs_recv, core_send, core_recv, lo_send, lo_recv, fin_send, fin_recv,
):
    r = lax.axis_index("replica")
    x = lax.axis_index("dp")
    m = lax.axis_index("mp")
    y = m // NZ
    z = lax.rem(m, NZ)
    a = y // 2
    b = lax.rem(y, 2)
    y_back = 2 * x + b
    c = lax.rem(r, 2)
    other_core = r + 1 - 2 * c
    other_lo = lax.rem(r + 2, 4)
    moves = a != x

    def at_z(step):
        return lax.rem(z + step, NZ)

    def at_y(step):
        return lax.rem(y + step + NY, NY)

    def at_x(step):
        return lax.rem(x + step, NX)

    barrier = pltpu.get_barrier_semaphore()
    for step in range(1, NZ):
        pl.semaphore_signal(barrier, inc=1, device_id={"mp": y * NZ + at_z(step)}, device_id_type=MESH)
    for step in range(1, NY):
        pl.semaphore_signal(barrier, inc=1, device_id={"mp": at_y(step) * NZ + z}, device_id_type=MESH)
    for step in range(1, NX):
        pl.semaphore_signal(barrier, inc=1, device_id={"dp": at_x(step)}, device_id_type=MESH)
    pl.semaphore_signal(barrier, inc=1, device_id={"replica": other_core}, device_id_type=MESH)
    pl.semaphore_signal(barrier, inc=1, device_id={"replica": other_lo}, device_id_type=MESH)

    @pl.when(moves)
    def _():
        pl.semaphore_signal(barrier, inc=1, device_id={"dp": a, "mp": y_back * NZ + z}, device_id_type=MESH)

    weight_copies = []
    for h in range(2):
        for i, (to, start, size) in enumerate(SEGMENTS):
            weight_copies.append(
                pltpu.make_async_copy(
                    w_hbm.at[pl.ds(h * HALF + start, size), :],
                    w.at[h, pl.ds(to, size), :],
                    w_sem.at[h, i],
                )
            )
    for copy in weight_copies:
        copy.start()

    values = tok_ref[...].astype(F32)
    mean = jnp.mean(values, axis=1, keepdims=True)
    squares = jnp.sum(jnp.square(values - mean), axis=1, keepdims=True)
    lane = lax.broadcasted_iota(jnp.int32, (TOK, 128), 1)
    table = jnp.where(lane == 0, mean, jnp.where(lane == 1, squares, 0.0))
    stats = jnp.transpose(table)[:8, :]
    stat_z_tx[...] = stats
    stat_z[pl.ds(z, 1)] = stats[None]

    pl.semaphore_wait(barrier, 15 + jnp.where(moves, 1, 0))

    copies = []
    for step in range(1, NZ):
        copies.append(
            remote(stat_z_tx, stat_z.at[z], stat_send.at[step], stat_recv.at[z], mp=y * NZ + at_z(step))
        )
        copies[-1].start()
    for step in range(1, NZ):
        remote(
            stat_z_tx, stat_z.at[at_z(step)], stat_send.at[step], stat_recv.at[at_z(step)], mp=y * NZ + at_z(step)
        ).wait_recv()
    stats = merge_stats(stat_z[...], float(FEAT))
    stat_tx[...] = stats
    stat_y[pl.ds(y, 1)] = stats[None]
    for step in range(1, NY):
        copies.append(
            remote(
                stat_tx, stat_y.at[y], stat_send.at[NZ + step], stat_recv.at[NZ + y], mp=at_y(step) * NZ + z
            )
        )
        copies[-1].start()
    for step in range(1, NY):
        remote(
            stat_tx, stat_y.at[at_y(step)], stat_send.at[NZ + step], stat_recv.at[NZ + at_y(step)],
            mp=at_y(step) * NZ + z,
        ).wait_recv()
    stats = merge_stats(stat_y[...], float(HALF))
    table = jnp.transpose(jnp.concatenate([stats, jnp.zeros((120, 128), F32)], axis=0))
    centre = table[:, 0:1]
    scale = lax.rsqrt(table[:, 1:2] * (1.0 / D) + 1e-06)
    normed = (values - centre) * scale * gain_ref[...].astype(F32)
    tail = jnp.concatenate([normed[:, 128:], jnp.zeros((TOK, 64), F32)], axis=1)
    block[0:TOK, :] = normed[:, :128].astype(BF16)
    block[TOK:FEAT, :] = jnp.where(
        lanes_below_64(SUB), tail[:SUB], pltpu.roll(tail[SUB:], 64, 1)
    ).astype(BF16)

    perm = remote(
        block, gathered.at[z], perm_send.at[0], perm_recv.at[0], dp=a, mp=y_back * NZ + z
    )

    @pl.when(moves)
    def _():
        perm.start()
        perm.wait_recv()

    @pl.when(jnp.logical_not(moves))
    def _():
        gathered[pl.ds(z, 1)] = block[...][None]

    for step in range(1, NZ):
        copies.append(
            remote(
                gathered.at[z], gathered.at[z], zg_send.at[step], zg_recv.at[z], mp=y * NZ + at_z(step)
            )
        )
        copies[-1].start()
    for step in range(1, NZ):
        remote(
            gathered.at[at_z(step)], gathered.at[at_z(step)], zg_send.at[step], zg_recv.at[at_z(step)],
            mp=y * NZ + at_z(step),
        ).wait_recv()
    low = lanes_below_64(SUB)
    for zz in range(NZ):
        rows[pl.ds(y, 1), :, zz * 128 : (zz + 1) * 128] = gathered[zz, 0:TOK, :][None]
    for pair in range(NZ // 2):
        first = gathered[2 * pair, TOK:FEAT, :].astype(F32)
        second = gathered[2 * pair + 1, TOK:FEAT, :].astype(F32)
        top = jnp.where(low, first, pltpu.roll(second, 64, 1))
        bottom = jnp.where(low, pltpu.roll(first, 64, 1), second)
        both = jnp.concatenate([top, bottom], axis=0).astype(BF16)
        rows[pl.ds(y, 1), :, 512 + pair * 128 : 640 + pair * 128] = both[None]

    def gather_copy(way, step, sub, source):
        piece = rows.at[source, pl.ds(sub * SUB, SUB), :]
        sign = 1 - 2 * way
        return remote(
            piece, piece, yg_send.at[way, step, sub], yg_recv.at[way, step, sub], mp=at_y(sign) * NZ + z
        )

    def transpose_row(source):
        where_to = pl.multiple_of((source // 2) * TOK, TOK)
        rows_t[pl.ds(lax.rem(source, 2), 1), :, pl.ds(where_to, TOK)] = jnp.transpose(rows[source])[None]

    def project(group, index):
        total = jnp.dot(rows[2 * group], w[0], preferred_element_type=F32) + jnp.dot(
            rows[2 * group + 1], w[1], preferred_element_type=F32
        )

        @pl.when(group == x)
        def _():
            proj_own[...] = total

        @pl.when(group != x)
        def _():
            proj_tx[index] = total.astype(BF16)
            remote(
                proj_tx.at[index], proj_rx.at[x], px_send.at[index], px_recv.at[x], dp=group
            ).start()

    for sub in range(2):
        for way in range(2):
            copies.append(gather_copy(way, 0, sub, y))
            copies[-1].start()
    sign = 1 - 2 * b
    for copy in weight_copies:
        copy.wait()
    transpose_row(y)
    for step in range(1, 5):
        for sub in range(2):
            for way in range(2):
                if step == 4 and sub != way:
                    continue
                source = at_y(-step if way == 0 else step)
                gather_copy(way, step - 1, sub, source).wait_recv()
                if step < 3 or (step == 3 and sub == way):
                    copies.append(gather_copy(way, step, sub, source))
                    copies[-1].start()
        completing = at_y(step * sign if step % 2 else -step * sign)
        project(completing // 2, step - 1)
        transpose_row(at_y(step))
        if step < 4:
            transpose_row(at_y(-step))

    for step in range(1, NX):
        remote(
            proj_tx.at[0], proj_rx.at[at_x(step)], px_send.at[0], px_recv.at[at_x(step)], dp=at_x(step)
        ).wait_recv()
    projected = proj_own[...]
    for step in range(1, NX):
        projected = projected + proj_rx[at_x(step)].astype(F32)
    linear = lax.broadcasted_iota(jnp.int32, (TOK, COLS), 1) < QKV
    normal_cdf = 0.5 * (1.0 + lax.erf(projected * 0.7071067811865476))
    density = jnp.exp(-0.5 * projected * projected) * 0.3989422804014327
    act_ref[...] = jnp.where(linear, projected, projected * normal_cdf).astype(BF16)
    slopes = jnp.where(linear, 1.0, normal_cdf + projected * density)
    inner[pl.ds(x, 1)] = (og_ref[...].astype(F32) * slopes).astype(BF16)[None]

    for step in range(1, NX):
        copies.append(
            remote(inner.at[x], inner.at[x], ix_send.at[step], ix_recv.at[x], dp=at_x(step))
        )
        copies[-1].start()
    for step in range(1, NX):
        remote(
            inner.at[at_x(step)], inner.at[at_x(step)], ix_send.at[step], ix_recv.at[at_x(step)], dp=at_x(step)
        ).wait_recv()
    every = inner[...].reshape(NX * TOK, COLS)

    def weight_piece(half, k):
        left = rows_t[half, k * CHUNK : (k + 1) * CHUNK, :]
        return jnp.dot(left, every, preferred_element_type=F32)

    pieces = HALF // CHUNK

    def core_copy(k):
        return remote(
            core_tx.at[k], core_rx.at[k], core_send.at[k], core_recv.at[k], replica=other_core
        )

    def lo_copy(k):
        return remote(lo_tx.at[k], lo_rx.at[k], lo_send.at[k], lo_recv.at[k], replica=other_lo)

    def done_copy(k, half):
        return remote(
            done.at[half, k], done.at[half, k], fin_send.at[k], fin_recv.at[k], replica=other_core
        )

    for k in range(pieces):
        core_tx[k] = weight_piece(1 - c, k).astype(BF16)
        core_copy(k).start()

    def fill_part(target):
        group, half = target // 2, lax.rem(target, 2)
        part[pl.ds(target, 1)] = lax.dot_general(
            inner[group], w[half], (((1,), (1,)), ((), ())), preferred_element_type=F32
        )[None]

    lax.fori_loop(0, NY, lambda i, carry: (fill_part(i), carry)[1], 0)

    def ring_copy(way, h, sub):
        piece = pl.ds(sub * SUB, SUB)
        sign = 1 - 2 * way
        return remote(
            ytx.at[way, h - 1, piece, :],
            yrx.at[way, h - 1, piece, :],
            ys_send.at[way, h - 1, sub],
            ys_recv.at[way, h - 1, sub],
            mp=at_y(sign) * NZ + z,
        )

    def ring_send(way, h, sub):
        sign = 1 - 2 * way
        piece = slice(sub * SUB, (sub + 1) * SUB)
        value = part[at_y(sign * h), piece, :]
        farthest = 4 if sub == way else 3
        if h < farthest:
            ring_copy(way, h + 1, sub).wait_recv()
            value = value + yrx[way, h, piece, :].astype(F32)
        ytx[way, h - 1, piece, :] = value.astype(BF16)
        copies.append(ring_copy(way, h, sub))
        copies[-1].start()

    ring_send(0, 4, 0)
    ring_send(1, 4, 1)
    ring_send(0, 3, 1)
    ring_send(1, 3, 0)

    def weight_stage(k):
        own = weight_piece(c, k)
        core_copy(k).wait_recv()
        own = own + core_rx[k].astype(F32)
        lo_tx[k] = own.astype(BF16)
        lo_copy(k).start()

    out_copies = []

    def out_copy(half, k, index):
        segments = [
            (i, s) for i, s in enumerate(SEGMENTS) if k * CHUNK <= s[0] < (k + 1) * CHUNK
        ]
        for i, (place, start, size) in segments:
            copy = pltpu.make_async_copy(
                done.at[half, k, pl.ds(place - k * CHUNK, size), :],
                wg_hbm.at[pl.ds(half * HALF + start, size), :],
                out_sem.at[index, i],
            )
            copy.start()
            out_copies.append(copy)

    def finish_stage(k):
        lo_copy(k).wait_recv()
        total = lo_tx[k].astype(F32) + lo_rx[k].astype(F32)
        done[pl.ds(c, 1), k] = (total * 0.25).astype(BF16)[None]
        done_copy(k, c).start()
        out_copy(c, k, 0)

    for k in range(pieces):
        weight_stage(k)
    ring_send(0, 3, 0)
    ring_send(1, 3, 1)
    ring_send(0, 2, 1)
    ring_send(1, 2, 0)
    ring_send(0, 2, 0)
    ring_send(1, 2, 1)
    ring_send(0, 1, 1)
    ring_send(1, 1, 0)
    finish_stage(0)
    ring_send(0, 1, 0)
    ring_send(1, 1, 1)
    finish_stage(1)
    for way, sub in ((0, 1), (1, 0), (0, 0), (1, 1)):
        ring_copy(way, 1, sub).wait_recv()
    total = part[y] + yrx[0, 0].astype(F32) + yrx[1, 0].astype(F32)

    for zz in range(NZ):
        first, packed = split_piece(total, zz)
        ztx[zz, 0:TOK, :] = first.astype(BF16)
        ztx[zz, TOK:FEAT, :] = packed.astype(BF16)
    for step in range(1, NZ):
        copies.append(
            remote(ztx.at[at_z(step)], zrx.at[z], zs_send.at[step], zs_recv.at[z], mp=y * NZ + at_z(step))
        )
        copies[-1].start()
    for step in range(1, NZ):
        remote(
            ztx.at[0], zrx.at[at_z(step)], zs_send.at[step], zs_recv.at[at_z(step)], mp=y * NZ + at_z(step)
        ).wait_recv()
    total = ztx[z].astype(F32)
    for step in range(1, NZ):
        total = total + zrx[at_z(step)].astype(F32)
    last_tx[...] = total.astype(BF16)
    back = remote(
        last_tx, last_rx, perm_send.at[1], perm_recv.at[1], dp=a, mp=y_back * NZ + z
    )

    @pl.when(moves)
    def _():
        back.start()

    finish_stage(2)

    @pl.when(moves)
    def _():
        back.wait_recv()

    @pl.when(jnp.logical_not(moves))
    def _():
        last_rx[...] = last_tx[...]

    ng_ref[:, 0:128] = last_rx[0:TOK, :]
    packed = last_rx[TOK:FEAT, :].astype(F32)
    ng_ref[0:SUB, 128:FEAT] = packed[:, :64].astype(BF16)
    ng_ref[SUB:TOK, 128:FEAT] = pltpu.roll(packed, 64, 1)[:, :64].astype(BF16)

    for k in range(pieces):
        done_copy(k, 1 - c).wait_recv()
        out_copy(1 - c, k, 1)

    @pl.when(moves)
    def _():
        perm.wait_send()
        back.wait_send()

    for index in range(4):
        step = index + 1
        group = at_y(step * sign if step % 2 else -step * sign) // 2

        @pl.when(group != x)
        def _():
            remote(
                proj_tx.at[index], proj_rx.at[x], px_send.at[index], px_recv.at[x], dp=group
            ).wait_send()

    for copy in copies:
        copy.wait_send()
    for k in range(pieces):
        core_copy(k).wait_send()
        lo_copy(k).wait_send()
        done_copy(k, c).wait_send()
    for copy in out_copies:
        copy.wait()


def local(tokens, norm_gain, joined_weight, output_grad):
    start = lax.axis_index("mp") * FEAT
    gain = lax.dynamic_slice(norm_gain, (start,), (FEAT,)).reshape(1, FEAT)
    vmem = pl.BlockSpec(memory_space=pltpu.VMEM)
    anywhere = pl.BlockSpec(memory_space=pl.ANY)
    dma = pltpu.SemaphoreType.DMA
    pieces = HALF // CHUNK
    scratch = [
        pltpu.VMEM((2, HALF, COLS), BF16),
        pltpu.VMEM((8, 128), F32),
        pltpu.VMEM((NZ, 8, 128), F32),
        pltpu.VMEM((NY, 8, 128), F32),
        pltpu.VMEM((8, 128), F32),
        pltpu.VMEM((FEAT, 128), BF16),
        pltpu.VMEM((NZ, FEAT, 128), BF16),
        pltpu.VMEM((NY, TOK, HALF), BF16),
        pltpu.VMEM((2, HALF, NX * TOK), BF16),
        pltpu.VMEM((NX, TOK, COLS), BF16),
        pltpu.VMEM((NX, TOK, COLS), BF16),
        pltpu.VMEM((TOK, COLS), F32),
        pltpu.VMEM((NX, TOK, COLS), BF16),
        pltpu.VMEM((NY, TOK, HALF), F32),
        pltpu.VMEM((2, 4, TOK, HALF), BF16),
        pltpu.VMEM((2, 4, TOK, HALF), BF16),
        pltpu.VMEM((NZ, FEAT, 128), BF16),
        pltpu.VMEM((NZ, FEAT, 128), BF16),
        pltpu.VMEM((FEAT, 128), BF16),
        pltpu.VMEM((FEAT, 128), BF16),
        pltpu.VMEM((pieces, CHUNK, COLS), BF16),
        pltpu.VMEM((pieces, CHUNK, COLS), BF16),
        pltpu.VMEM((pieces, CHUNK, COLS), BF16),
        pltpu.VMEM((pieces, CHUNK, COLS), BF16),
        pltpu.VMEM((2, pieces, CHUNK, COLS), BF16),
        dma((2, 8)),
        dma((2, 8)),
        dma((NZ + NY,)),
        dma((NZ + NY,)),
        dma((2,)),
        dma((2,)),
        dma((NZ,)),
        dma((NZ,)),
        dma((2, 4, 2)),
        dma((2, 4, 2)),
        dma((NX,)),
        dma((NX,)),
        dma((NX,)),
        dma((NX,)),
        dma((2, 4, 2)),
        dma((2, 4, 2)),
        dma((NZ,)),
        dma((NZ,)),
        dma((pieces,)),
        dma((pieces,)),
        dma((pieces,)),
        dma((pieces,)),
        dma((pieces,)),
        dma((pieces,)),
    ]
    return pl.pallas_call(
        kernel,
        out_shape=(
            jax.ShapeDtypeStruct((TOK, COLS), BF16),
            jax.ShapeDtypeStruct((TOK, FEAT), BF16),
            jax.ShapeDtypeStruct((2 * HALF, COLS), BF16),
        ),
        in_specs=[vmem, vmem, vmem, anywhere],
        out_specs=(vmem, vmem, anywhere),
        scratch_shapes=scratch,
        compiler_params=pltpu.CompilerParams(
            collective_id=0, has_side_effects=True, vmem_limit_bytes=56 * 1024 * 1024
        ),
        cost_estimate=pl.CostEstimate(flops=3200000000, bytes_accessed=5000000, transcendentals=200000),
    )(tokens, gain, output_grad, joined_weight)


def solution(mesh):
    in_specs = (P(("replica", "dp"), "mp"), P(), P("dp", "mp"), P(("replica", "dp"), "mp"))
    out_specs = (P(("replica", "dp"), "mp"), P(("replica", "dp"), "mp"), P("dp", "mp"))
    return jax.shard_map(local, mesh=mesh, in_specs=in_specs, out_specs=out_specs, check_vma=False)
```

```python
import jax
import jax.numpy as jnp
from jax import lax
from jax.experimental import pallas as pl
from jax.experimental.pallas import tpu as pltpu
from jax.sharding import PartitionSpec as P

MESH = pl.DeviceIdType.MESH
F32 = jnp.float32
BF16 = jnp.bfloat16

NX = 4
NY = 8
NZ = 4
TOK = 128
FEAT = 192
HALF = NZ * FEAT
COLS = 672
QKV = 288
D = 6144
CHUNK = 256
PIECES = HALF // CHUNK


def remote(src, dst, send_sem, recv_sem, **device):
    return pltpu.make_async_remote_copy(
        src_ref=src,
        dst_ref=dst,
        send_sem=send_sem,
        recv_sem=recv_sem,
        device_id=device,
        device_id_type=MESH,
    )


def merge_stats(stack, features):
    count = stack.shape[0]
    means = stack[:, 0:1, :]
    mean = jnp.sum(means, axis=0) / count
    squares = jnp.sum(stack[:, 1:2, :], axis=0) + features * jnp.sum(
        jnp.square(means - mean[None]), axis=0
    )
    return stats_table(mean, squares)


def stats_table(mean, squares):
    row = lax.broadcasted_iota(jnp.int32, (8, 128), 0)
    return jnp.where(row == 0, mean, jnp.where(row == 1, squares, 0.0))


def kernel(
    tok_ref, gain_ref, og_hbm, w_hbm, act_ref, ng_ref, wg_hbm,
    w, w_turned, og, gain_rows, gain, stat_z_tx, stat_y_tx, stat_z, stat_y, stat_x, rows, normed,
    site_rows, proj_tx, proj_rx, proj_own, inner, part, ytx, yrx, ztx, zrx, last_tx,
    w_sum, done,
    w_sem, out_sem, stat_send, stat_recv, perm_send, perm_recv, zg_send, zg_recv,
    yg_send, yg_recv, site_send, site_recv, px_send, px_recv, ix_send, lo_send, core_send, inner_recv,
    ys_send, ys_recv, zs_send, zs_recv, fin_send, fin_recv,
):
    r = lax.axis_index("replica")
    x = lax.axis_index("dp")
    m = lax.axis_index("mp")
    y = m // NZ
    z = lax.rem(m, NZ)
    a = y // 2
    b = lax.rem(y, 2)
    y_back = 2 * x + b
    c = lax.rem(r, 2)
    other_core = r + 1 - 2 * c
    other_lo = lax.rem(r + 2, 4)
    across = 3 - r
    moves = a != x

    def at_z(step):
        return lax.rem(z + step, NZ)

    def at_y(step):
        return lax.rem(y + step + NY, NY)

    def at_x(step):
        return lax.rem(x + step, NX)

    def mp(y_place, z_place):
        return y_place * NZ + z_place

    copies = []

    def start(copy):
        copies.append(copy)
        copy.start()

    barrier = pltpu.get_barrier_semaphore()
    greeted = [{"mp": mp(y, at_z(step))} for step in range(1, NZ)]
    greeted += [{"mp": mp(at_y(step), z)} for step in range(1, NY)]
    greeted += [{"dp": at_x(step)} for step in range(1, NX)]
    greeted += [{"replica": other_core}, {"replica": other_lo}, {"replica": across}]
    for device in greeted:
        pl.semaphore_signal(barrier, inc=1, device_id=device, device_id_type=MESH)

    @pl.when(moves)
    def _():
        pl.semaphore_signal(
            barrier, inc=1, device_id={"dp": a, "mp": mp(y_back, z)}, device_id_type=MESH
        )

    w_copy = pltpu.make_async_copy(w_hbm, w, w_sem.at[0])
    og_copy = pltpu.make_async_copy(og_hbm, og, w_sem.at[1])
    w_copy.start()
    og_copy.start()

    values = tok_ref[...].astype(F32)
    mean = jnp.mean(values, axis=0, keepdims=True)
    squares = jnp.sum(jnp.square(values - mean), axis=0, keepdims=True)
    stats = stats_table(mean, squares)
    stat_z_tx[...] = stats
    stat_z[pl.ds(z, 1)] = stats[None]

    pl.semaphore_wait(barrier, len(greeted) + jnp.where(moves, 1, 0))

    def z_block(source_y, source_z):
        return rows.at[source_y, pl.ds(pl.multiple_of(source_z * FEAT, FEAT), FEAT), :]

    def perm_copy():
        return remote(
            tok_ref, z_block(y_back, z), perm_send.at[0], perm_recv.at[0], dp=a, mp=mp(y_back, z)
        )

    def back_copy():
        return remote(
            last_tx, ng_ref, perm_send.at[1], perm_recv.at[1], dp=a, mp=mp(y_back, z)
        )

    def stat_z_copy(step, slot):
        return remote(
            stat_z_tx, stat_z.at[slot], stat_send.at[step], stat_recv.at[slot], mp=mp(y, at_z(step))
        )

    def stat_y_copy(step, slot):
        return remote(
            stat_y_tx, stat_y.at[slot], stat_send.at[NZ + step], stat_recv.at[NZ + slot],
            mp=mp(at_y(step), z),
        )

    def stat_x_copy(step, slot):
        return remote(
            stat_x.at[slot], stat_x.at[slot], stat_send.at[NZ + NY + step],
            stat_recv.at[NZ + NY + slot], dp=at_x(step),
        )

    @pl.when(moves)
    def _():
        perm_copy().start()

    for step in range(1, NZ):
        start(stat_z_copy(step, z))

    @pl.when(jnp.logical_not(moves))
    def _():
        rows[pl.ds(y, 1), pl.ds(pl.multiple_of(z * FEAT, FEAT), FEAT), :] = tok_ref[...][None]

    gain_rows[...] = gain_ref[...].astype(F32)
    table = jnp.transpose(
        jnp.concatenate([gain_rows[pl.ds(12 * x, 12), :], jnp.zeros((116, 128), F32)], axis=0)
    )
    for i in range(12):
        gain[i * 128 : (i + 1) * 128, :] = jnp.broadcast_to(table[:, i : i + 1], (128, 128))

    for step in range(1, NZ):
        stat_z_copy(step, at_z(step)).wait_recv()
    stats = merge_stats(stat_z[...], float(FEAT))
    stat_y_tx[...] = stats
    stat_y[pl.ds(y, 1)] = stats[None]
    for step in range(1, NY):
        start(stat_y_copy(step, y))

    @pl.when(moves)
    def _():
        perm_copy().wait_recv()


    def gather_z(step, source):
        piece = z_block(y, source)
        return remote(piece, piece, zg_send.at[step], zg_recv.at[source], mp=mp(y, at_z(step)))

    def gather_y(way, step, k, source):
        piece = z_block(source, at_z(k))
        return remote(
            piece, piece, yg_send.at[way, step, k], yg_recv.at[way, step, k],
            mp=mp(at_y(1 - 2 * way), z),
        )

    for step in range(1, NZ):
        start(gather_z(step, z))
    for way in range(2):
        start(gather_y(way, 0, 0, y))
    for step in range(1, NY):
        stat_y_copy(step, at_y(step)).wait_recv()
    stat_x[pl.ds(x, 1)] = merge_stats(stat_y[...], float(HALF))[None]
    for step in range(1, NX):
        start(stat_x_copy(step, x))
    for k in range(1, NZ):
        gather_z(k, at_z(k)).wait_recv()
        for way in range(2):
            start(gather_y(way, 0, k, y))
    w_copy.wait()

    def turn(piece):
        columns = slice(piece * HALF // 2, (piece + 1) * HALF // 2)
        w_turned[columns, :] = jnp.transpose(w[:, columns])

    turn(0)
    for step in range(1, NX):
        stat_x_copy(step, at_x(step)).wait_recv()

    def site_copy(t, replica):
        return remote(
            normed.at[t], site_rows.at[r, t // 2], site_send.at[replica // 2, t],
            site_recv.at[r, t // 2], replica=replica,
        )

    def normalize(t):
        h = lax.rem(t, 2)
        statistics = stat_x[t // 2]
        scale = lax.rsqrt(statistics[1:2] * (1.0 / D) + 1e-06)
        column = gain[pl.ds(pl.multiple_of(h * HALF, HALF), HALF), :]
        value = (rows[t].astype(F32) - statistics[0:1]) * scale * column
        normed[pl.ds(t, 1)] = value.astype(BF16)[None]
        start(site_copy(t, 2 * (1 - r // 2) + h))

        @pl.when(h != c)
        def _():
            site_copy(t, other_core).start()

    def project(group, index):
        total = jnp.dot(w[:, :HALF], normed[2 * group], preferred_element_type=F32) + jnp.dot(
            w[:, HALF:], normed[2 * group + 1], preferred_element_type=F32
        )

        @pl.when(group == x)
        def _():
            proj_own[...] = total

        @pl.when(group != x)
        def _():
            proj_tx[index] = total.astype(BF16)
            proj_copy(group, index).start()

    def proj_copy(group, index):
        return remote(
            proj_tx.at[index], proj_rx.at[x], px_send.at[index], px_recv.at[x], dp=group
        )

    sign = 1 - 2 * b

    def completed(step):
        return at_y(step * sign if step % 2 else -step * sign) // 2

    normalize(y)
    for step in range(1, 5):
        for k in range(NZ):
            for way in range(2):
                if step == 4 and k % 2 != way:
                    continue
                source = at_y(-step if way == 0 else step)
                gather_y(way, step - 1, k, source).wait_recv()
                if step < 3 or (step == 3 and k % 2 == way):
                    start(gather_y(way, step, k, source))
        normalize(at_y(step))
        if step < 4:
            normalize(at_y(-step))
        project(completed(step), step - 1)
        if step < 4:
            turn(step)

    for step in range(1, NX):
        remote(
            proj_tx.at[0], proj_rx.at[at_x(step)], px_send.at[0], px_recv.at[at_x(step)], dp=at_x(step)
        ).wait_recv()
    projected = proj_own[...]
    for step in range(1, NX):
        projected = projected + proj_rx[at_x(step)].astype(F32)
    og_copy.wait()
    act_ref[0:QKV, :] = projected[0:QKV].astype(BF16)
    inner[pl.ds(r, 1), pl.ds(x, 1), 0:QKV, :] = og[0:QKV, :][None, None]
    hidden = projected[QKV:]
    normal_cdf = 0.5 * (1.0 + lax.erf(hidden * 0.7071067811865476))
    density = jnp.exp(-0.5 * hidden * hidden) * 0.3989422804014327
    act_ref[QKV:, :] = (hidden * normal_cdf).astype(BF16)
    inner[pl.ds(r, 1), pl.ds(x, 1), QKV:, :] = (
        og[QKV:, :].astype(F32) * (normal_cdf + hidden * density)
    ).astype(BF16)[None, None]

    def inner_x(step, source):
        piece = inner.at[r, source]
        return remote(piece, piece, ix_send.at[step], inner_recv.at[r, source], dp=at_x(step))

    def inner_lo(replica, group):
        piece = inner.at[replica, group]
        return remote(
            piece, piece, lo_send.at[group], inner_recv.at[replica, group], replica=other_lo
        )

    def inner_core(replica, group):
        piece = inner.at[replica, group]
        return remote(
            piece, piece, core_send.at[replica // 2, group], inner_recv.at[replica, group],
            replica=other_core,
        )

    for step in range(1, NX):
        start(inner_x(step, x))
    start(inner_lo(r, x))
    start(inner_core(r, x))
    for step in (1, 3, 2):
        inner_x(step, at_x(step)).wait_recv()
        start(inner_lo(r, at_x(step)))
        start(inner_core(r, at_x(step)))

    def every(replica):
        return jnp.concatenate([inner[replica, g] for g in range(NX)], axis=1)


    part[...] = jnp.dot(w_turned[...], every(r), preferred_element_type=F32)

    def part_of(target, k):
        start_row = pl.multiple_of(lax.rem(target, 2) * HALF + at_z(k) * FEAT, FEAT)
        lane = pl.multiple_of((target // 2) * TOK, TOK)
        return part[pl.ds(start_row, FEAT), pl.ds(lane, TOK)]

    def ring_copy(way, h, k):
        return remote(
            ytx.at[way, h - 1, k],
            yrx.at[way, h - 1, k],
            ys_send.at[way, h - 1, k],
            ys_recv.at[way, h - 1, k],
            mp=mp(at_y(1 - 2 * way), z),
        )

    def ring_send(way, h, k):
        value = part_of(at_y((1 - 2 * way) * h), k)
        if h < (4 if k % 2 == way else 3):
            ring_copy(way, h + 1, k).wait_recv()
            value = value + yrx[way, h, k].astype(F32)
        ytx[way, h - 1, k] = value.astype(BF16)
        start(ring_copy(way, h, k))

    def ring_round(h, ks):
        for k in ks:
            for way in range(2):
                if h < 4 or k % 2 == way:
                    ring_send(way, h, k)

    def rows_of(replica, piece):
        return jnp.concatenate([site_rows[replica, g, piece, :] for g in range(NX)], axis=1)

    def own_rows(piece):
        return jnp.concatenate([normed[2 * g + c, piece, :] for g in range(NX)], axis=1)

    def weight_piece(left, right):
        return lax.dot_general(left, right, (((1,), (1,)), ((), ())), preferred_element_type=F32)

    def add_weight(replica):
        for g in range(NX):
            remote(
                normed.at[0], site_rows.at[replica, g], site_send.at[0, 0], site_recv.at[replica, g],
                replica=other_core,
            ).wait_recv()
        left = every(replica)
        for k in range(PIECES):
            piece = slice(k * CHUNK, (k + 1) * CHUNK)
            w_sum[k] += weight_piece(left, rows_of(replica, piece))

    def wait_inner(replica):
        for g in range(NX):
            inner_core(replica, g).wait_recv()

    def pass_on(step):
        inner_lo(other_lo, at_x(step)).wait_recv()
        start(inner_core(other_lo, at_x(step)))

    def done_copy(k, half):
        return remote(
            done.at[half, k], done.at[half, k], fin_send.at[k], fin_recv.at[k], replica=other_core
        )

    out_copies = []

    def out_copy(half, k, index):
        copy = pltpu.make_async_copy(
            done.at[half, k],
            wg_hbm.at[:, pl.ds(pl.multiple_of(half * HALF + k * CHUNK, CHUNK), CHUNK)],
            out_sem.at[index, k],
        )
        copy.start()
        out_copies.append(copy)

    order = (1, 3, 2, 0)
    ring_round(4, order)
    for k in order:
        for way in range(2):
            if k % 2 != way:
                ring_send(way, 3, k)
    for k in range(PIECES):
        w_sum[k] = weight_piece(every(r), own_rows(slice(k * CHUNK, (k + 1) * CHUNK)))
    pass_on(0)
    for k in order:
        for way in range(2):
            if k % 2 == way:
                ring_send(way, 3, k)
    wait_inner(other_core)
    add_weight(other_core)
    ring_round(2, order[:2])
    pass_on(1)
    ring_round(2, order[2:])
    pass_on(3)
    ring_round(1, order[:2])
    pass_on(2)
    ring_round(1, order[2:])
    add_weight(other_lo)

    def scatter_z(step, source):
        return remote(
            ztx.at[step], zrx.at[source], zs_send.at[step], zs_recv.at[source], mp=mp(y, at_z(step))
        )

    for k in order:
        for way in range(2):
            ring_copy(way, 1, k).wait_recv()
        total = part_of(y, k) + yrx[0, 0, k].astype(F32) + yrx[1, 0, k].astype(F32)
        if k:
            ztx[k] = total.astype(BF16)
            start(scatter_z(k, z))
    wait_inner(across)
    add_weight(across)
    for step in range(1, NZ):
        scatter_z(step, at_z(step)).wait_recv()
        total = total + zrx[at_z(step)].astype(F32)

    @pl.when(moves)
    def _():
        last_tx[...] = total.astype(BF16)
        back_copy().start()

    @pl.when(jnp.logical_not(moves))
    def _():
        ng_ref[...] = total.astype(BF16)

    for k in range(PIECES):
        done[pl.ds(c, 1), k] = (w_sum[k] * 0.25).astype(BF16)[None]
        start(done_copy(k, c))
        out_copy(c, k, 0)
    for k in range(PIECES):
        done_copy(k, 1 - c).wait_recv()
        out_copy(1 - c, k, 1)

    @pl.when(moves)
    def _():
        back_copy().wait_recv()
        back_copy().wait_send()
        perm_copy().wait_send()

    for index in range(NX):
        @pl.when(completed(index + 1) != x)
        def _(index=index):
            proj_copy(completed(index + 1), index).wait_send()

    for g in range(NX):
        site_copy(2 * g + 1 - c, other_core).wait_send()
    for copy in copies:
        copy.wait_send()
    for copy in out_copies:
        copy.wait()


def hand_over(act_in, ng_in, wg_in, act_out, ng_out, wg_out, act, ng, wg, sem):
    pieces = [(act_in, act, act_out), (ng_in, ng, ng_out)]
    for i in range(6):
        piece = pl.ds(i * 112, 112)
        pieces.append((wg_in.at[piece, :], wg.at[piece, :], wg_out.at[piece, :]))
    loads = [
        pltpu.make_async_copy(source, held, sem.at[0, i]) for i, (source, held, _) in enumerate(pieces)
    ]
    stores = [
        pltpu.make_async_copy(held, target, sem.at[1, i]) for i, (_, held, target) in enumerate(pieces)
    ]
    for load in loads:
        load.start()
    for load, store in zip(loads, stores):
        load.wait()
        store.start()
    for store in stores:
        store.wait()


def local(tokens, norm_gain, joined_weight, output_grad):
    vmem = pl.BlockSpec(memory_space=pltpu.VMEM)
    anywhere = pl.BlockSpec(memory_space=pl.ANY)
    dma = pltpu.SemaphoreType.DMA
    scratch = [
        pltpu.VMEM((COLS, 2 * HALF), BF16),
        pltpu.VMEM((2 * HALF, COLS), BF16),
        pltpu.VMEM((COLS, TOK), BF16),
        pltpu.VMEM((D // 128, 128), F32),
        pltpu.VMEM((2 * HALF, TOK), F32),
        pltpu.VMEM((8, 128), F32),
        pltpu.VMEM((8, 128), F32),
        pltpu.VMEM((NZ, 8, 128), F32),
        pltpu.VMEM((NY, 8, 128), F32),
        pltpu.VMEM((NX, 8, 128), F32),
        pltpu.VMEM((NY, HALF, TOK), BF16),
        pltpu.VMEM((NY, HALF, TOK), BF16),
        pltpu.VMEM((4, NX, HALF, TOK), BF16),
        pltpu.VMEM((NX, COLS, TOK), BF16),
        pltpu.VMEM((NX, COLS, TOK), BF16),
        pltpu.VMEM((COLS, TOK), F32),
        pltpu.VMEM((4, NX, COLS, TOK), BF16),
        pltpu.VMEM((2 * HALF, NX * TOK), F32),
        pltpu.VMEM((2, 4, NZ, FEAT, TOK), BF16),
        pltpu.VMEM((2, 4, NZ, FEAT, TOK), BF16),
        pltpu.VMEM((NZ, FEAT, TOK), BF16),
        pltpu.VMEM((NZ, FEAT, TOK), BF16),
        pltpu.VMEM((FEAT, TOK), BF16),
        pltpu.VMEM((PIECES, COLS, CHUNK), F32),
        pltpu.VMEM((2, PIECES, COLS, CHUNK), BF16),
        dma((2,)),
        dma((2, PIECES)),
        dma((NZ + NY + NX,)),
        dma((NZ + NY + NX,)),
        dma((2,)),
        dma((2,)),
        dma((NZ,)),
        dma((NZ,)),
        dma((2, 4, NZ)),
        dma((2, 4, NZ)),
        dma((2, NY)),
        dma((4, NX)),
        dma((NX,)),
        dma((NX,)),
        dma((NX,)),
        dma((NX,)),
        dma((2, NX)),
        dma((4, NX)),
        dma((2, 4, NZ)),
        dma((2, 4, NZ)),
        dma((NZ,)),
        dma((NZ,)),
        dma((PIECES,)),
        dma((PIECES,)),
    ]
    shapes = (
        jax.ShapeDtypeStruct((COLS, TOK), BF16),
        jax.ShapeDtypeStruct((FEAT, TOK), BF16),
        jax.ShapeDtypeStruct((COLS, 2 * HALF), BF16),
    )
    results = pl.pallas_call(
        kernel,
        out_shape=shapes,
        in_specs=[vmem, vmem, anywhere, anywhere],
        out_specs=(vmem, vmem, anywhere),
        scratch_shapes=scratch,
        compiler_params=pltpu.CompilerParams(
            collective_id=0, has_side_effects=True, vmem_limit_bytes=56 * 1024 * 1024
        ),
        cost_estimate=pl.CostEstimate(flops=3200000000, bytes_accessed=5000000, transcendentals=200000),
    )(
        tokens.T,
        norm_gain.reshape(D // 128, 128),
        output_grad.T,
        joined_weight.T,
    )
    activated, normed_grad, weight_grad = pl.pallas_call(
        hand_over,
        out_shape=shapes,
        in_specs=[anywhere] * 3,
        out_specs=(anywhere,) * 3,
        scratch_shapes=[pltpu.VMEM(shape.shape, BF16) for shape in shapes] + [dma((2, 8))],
        cost_estimate=pl.CostEstimate(flops=0, bytes_accessed=4600000, transcendentals=0),
    )(*results)
    return activated.T, normed_grad.T, weight_grad.T


def solution(mesh):
    in_specs = (P(("replica", "dp"), "mp"), P(), P("dp", "mp"), P(("replica", "dp"), "mp"))
    out_specs = (P(("replica", "dp"), "mp"), P(("replica", "dp"), "mp"), P("dp", "mp"))
    return jax.shard_map(local, mesh=mesh, in_specs=in_specs, out_specs=out_specs, check_vma=False)
```

```python
import jax
import jax.numpy as jnp
from jax import lax
from jax.experimental import pallas as pl
from jax.experimental.pallas import tpu as pltpu
from jax.sharding import PartitionSpec as P

MESH = pl.DeviceIdType.MESH
F32 = jnp.float32
BF16 = jnp.bfloat16

NX = 4
NY = 8
NZ = 4
TOK = 128
FEAT = 192
HALF = NZ * FEAT
COLS = 672
QKV = 288
D = 6144
CHUNK = 256
PIECES = HALF // CHUNK
FAR = 2
PARTS = 3
PART = COLS // PARTS


def remote(src, dst, send_sem, recv_sem, **device):
    return pltpu.make_async_remote_copy(
        src_ref=src,
        dst_ref=dst,
        send_sem=send_sem,
        recv_sem=recv_sem,
        device_id=device,
        device_id_type=MESH,
    )


def merge_stats(stack, features):
    count = stack.shape[0]
    means = stack[:, 0:1, :]
    mean = jnp.sum(means, axis=0) / count
    squares = jnp.sum(stack[:, 1:2, :], axis=0) + features * jnp.sum(
        jnp.square(means - mean[None]), axis=0
    )
    return stats_table(mean, squares)


def stats_table(mean, squares):
    row = lax.broadcasted_iota(jnp.int32, (8, 128), 0)
    return jnp.where(row == 0, mean, jnp.where(row == 1, squares, 0.0))


def kernel(
    tok_ref, gain_ref, og_hbm, w_hbm, act_ref, ng_ref, wg_hbm,
    w, w_turned, og, gain_rows, gain, stat_z_tx, stat_y_tx, stat_z, stat_y, stat_x, rows, normed,
    site_rows, proj_tx, proj_rx, proj_own, inner, part, ytx, yrx, ztx, zrx, last_tx,
    w_sum, w_far, lo_tx, lo_rx, done,
    w_sem, out_sem, stat_send, stat_recv, perm_send, perm_recv, zg_send, zg_recv,
    yg_send, yg_recv, site_send, site_recv, px_send, px_recv, ix_send, ix_recv, lo_send, core_send, inner_recv,
    ys_send, ys_recv, zs_send, zs_recv, sum_send, sum_recv, fin_send, fin_recv,
):
    r = lax.axis_index("replica")
    x = lax.axis_index("dp")
    m = lax.axis_index("mp")
    y = m // NZ
    z = lax.rem(m, NZ)
    a = y // 2
    b = lax.rem(y, 2)
    y_back = 2 * x + b
    back_x = lax.rem(a + 2, NX)
    from_y = 2 * lax.rem(x + 2, NX) + b
    c = lax.rem(r, 2)
    other_core = r + 1 - 2 * c
    other_lo = lax.rem(r + 2, 4)
    across = 3 - r
    moves = a != x

    def at_z(step):
        return lax.rem(z + step, NZ)

    def at_y(step):
        return lax.rem(y + step + NY, NY)

    def at_x(step):
        return lax.rem(x + step, NX)

    def mp(y_place, z_place):
        return y_place * NZ + z_place

    copies = []

    def start(copy):
        copies.append(copy)
        copy.start()

    barrier = pltpu.get_barrier_semaphore()
    greeted = [{"mp": mp(y, at_z(step))} for step in range(1, NZ)]
    greeted += [{"mp": mp(at_y(step), z)} for step in range(1, NY)]
    greeted += [{"dp": at_x(step)} for step in range(1, NX)]
    greeted += [{"replica": other_core}, {"replica": other_lo}, {"replica": across}]
    greeted += [{"dp": a, "mp": mp(from_y, z)}]
    for device in greeted:
        pl.semaphore_signal(barrier, inc=1, device_id=device, device_id_type=MESH)

    @pl.when(moves)
    def _():
        pl.semaphore_signal(
            barrier, inc=1, device_id={"dp": a, "mp": mp(y_back, z)}, device_id_type=MESH
        )

    w_copy = pltpu.make_async_copy(w_hbm, w, w_sem.at[0])
    og_copy = pltpu.make_async_copy(og_hbm, og, w_sem.at[1])
    w_copy.start()
    og_copy.start()

    values = tok_ref[...].astype(F32)
    mean = jnp.mean(values, axis=0, keepdims=True)
    squares = jnp.sum(jnp.square(values - mean), axis=0, keepdims=True)
    stats = stats_table(mean, squares)
    stat_z_tx[...] = stats
    stat_z[pl.ds(z, 1)] = stats[None]

    pl.semaphore_wait(barrier, len(greeted) + jnp.where(moves, 1, 0))

    def z_block(source_y, source_z):
        return rows.at[source_y, pl.ds(pl.multiple_of(source_z * FEAT, FEAT), FEAT), :]

    def perm_copy():
        return remote(
            tok_ref, z_block(y_back, z), perm_send.at[0], perm_recv.at[0], dp=a, mp=mp(y_back, z)
        )

    def stat_z_copy(step, slot):
        return remote(
            stat_z_tx, stat_z.at[slot], stat_send.at[step], stat_recv.at[slot], mp=mp(y, at_z(step))
        )

    def stat_y_copy(step, slot):
        return remote(
            stat_y_tx, stat_y.at[slot], stat_send.at[NZ + step], stat_recv.at[NZ + slot],
            mp=mp(at_y(step), z),
        )

    def stat_x_copy(step, slot):
        return remote(
            stat_x.at[slot], stat_x.at[slot], stat_send.at[NZ + NY + step],
            stat_recv.at[NZ + NY + slot], dp=at_x(step),
        )

    @pl.when(moves)
    def _():
        perm_copy().start()

    for step in range(1, NZ):
        start(stat_z_copy(step, z))

    @pl.when(jnp.logical_not(moves))
    def _():
        rows[pl.ds(y, 1), pl.ds(pl.multiple_of(z * FEAT, FEAT), FEAT), :] = tok_ref[...][None]

    gain_rows[...] = gain_ref[...].astype(F32)
    table = jnp.transpose(
        jnp.concatenate([gain_rows[pl.ds(12 * x, 12), :], jnp.zeros((116, 128), F32)], axis=0)
    )
    for i in range(12):
        gain[i * 128 : (i + 1) * 128, :] = jnp.broadcast_to(table[:, i : i + 1], (128, 128))

    for step in range(1, NZ):
        stat_z_copy(step, at_z(step)).wait_recv()
    stats = merge_stats(stat_z[...], float(FEAT))
    stat_y_tx[...] = stats
    stat_y[pl.ds(y, 1)] = stats[None]
    for step in range(1, NY):
        start(stat_y_copy(step, y))

    @pl.when(moves)
    def _():
        perm_copy().wait_recv()


    def gather_z(step, source):
        piece = z_block(y, source)
        return remote(piece, piece, zg_send.at[step], zg_recv.at[source], mp=mp(y, at_z(step)))

    def gather_y(way, step, k, source):
        piece = z_block(source, at_z(k))
        return remote(
            piece, piece, yg_send.at[way, step, k], yg_recv.at[way, step, k],
            mp=mp(at_y(1 - 2 * way), z),
        )

    for step in range(1, NZ):
        start(gather_z(step, z))
    for way in range(2):
        start(gather_y(way, 0, 0, y))
    for step in range(1, NY):
        stat_y_copy(step, at_y(step)).wait_recv()
    stat_x[pl.ds(x, 1)] = merge_stats(stat_y[...], float(HALF))[None]
    for step in range(1, NX):
        start(stat_x_copy(step, x))
    for k in range(1, NZ):
        gather_z(k, at_z(k)).wait_recv()
        for way in range(2):
            start(gather_y(way, 0, k, y))
    w_copy.wait()

    def turn(piece):
        columns = slice(piece * HALF // 2, (piece + 1) * HALF // 2)
        w_turned[columns, :] = jnp.transpose(w[:, columns])

    turn(0)
    for step in range(1, NX):
        stat_x_copy(step, at_x(step)).wait_recv()

    def site_copy(source, t, replica, features):
        piece = pl.ds(0, features)
        return remote(
            normed.at[t, piece, :], site_rows.at[source, t // 2, piece, :],
            site_send.at[replica // 2, t], site_recv.at[source, t // 2], replica=replica,
        )

    def normalize(t):
        h = lax.rem(t, 2)
        statistics = stat_x[t // 2]
        scale = lax.rsqrt(statistics[1:2] * (1.0 / D) + 1e-06)
        column = gain[pl.ds(pl.multiple_of(h * HALF, HALF), HALF), :]
        value = (rows[t].astype(F32) - statistics[0:1]) * scale * column
        normed[pl.ds(t, 1)] = value.astype(BF16)[None]
        start(site_copy(r, t, 2 * (1 - r // 2) + h, FAR * CHUNK))

        @pl.when(h != c)
        def _():
            site_copy(r, t, other_core, HALF).start()

    def project(group, index):
        for i in range(PARTS):
            columns = slice(i * PART, (i + 1) * PART)
            total = jnp.dot(
                w[columns, :HALF], normed[2 * group], preferred_element_type=F32
            ) + jnp.dot(w[columns, HALF:], normed[2 * group + 1], preferred_element_type=F32)

            @pl.when(group == x)
            def _(columns=columns, total=total):
                proj_own[columns, :] = total

            @pl.when(group != x)
            def _(i=i, columns=columns, total=total):
                proj_tx[index, columns, :] = total.astype(BF16)
                proj_copy(group, index, i).start()

    def proj_copy(group, index, i):
        columns = pl.ds(i * PART, PART)
        return remote(
            proj_tx.at[index, columns, :], proj_rx.at[x, columns, :],
            px_send.at[index, i], px_recv.at[x, i], dp=group,
        )

    def proj_wait(source, i):
        columns = pl.ds(i * PART, PART)
        remote(
            proj_tx.at[0, columns, :], proj_rx.at[source, columns, :],
            px_send.at[0, i], px_recv.at[source, i], dp=source,
        ).wait_recv()

    def activate_rows(low, high):
        columns = slice(low, high)
        projected = proj_own[columns, :]
        for step in range(1, NX):
            projected = projected + proj_rx[at_x(step), columns, :].astype(F32)
        if high <= QKV:
            act_ref[columns, :] = projected.astype(BF16)
            inner[pl.ds(r, 1), pl.ds(x, 1), columns, :] = og[columns, :][None, None]
        else:
            normal_cdf = 0.5 * (1.0 + lax.erf(projected * 0.7071067811865476))
            density = jnp.exp(-0.5 * projected * projected) * 0.3989422804014327
            act_ref[columns, :] = (projected * normal_cdf).astype(BF16)
            inner[pl.ds(r, 1), pl.ds(x, 1), columns, :] = (
                og[columns, :].astype(F32) * (normal_cdf + projected * density)
            ).astype(BF16)[None, None]

    def inner_x(step, source, i):
        piece = inner.at[r, source, pl.ds(i * PART, PART), :]
        return remote(piece, piece, ix_send.at[step, i], ix_recv.at[source, i], dp=at_x(step))

    def activate(step):
        @pl.when(completed(step) == x)
        def _():
            for i in range(PARTS):
                for other in range(1, NX):
                    proj_wait(at_x(other), i)
                cuts = [i * PART, (i + 1) * PART]
                if cuts[0] < QKV < cuts[1]:
                    cuts.insert(1, QKV)
                for low, high in zip(cuts[:-1], cuts[1:]):
                    activate_rows(low, high)
                for other in range(1, NX):
                    inner_x(other, x, i).start()

    sign = 1 - 2 * b

    def completed(step):
        return at_y(step * sign if step % 2 else -step * sign) // 2

    normalize(y)
    for step in range(1, 5):
        for k in range(NZ):
            for way in range(2):
                if step == 4 and k % 2 != way:
                    continue
                source = at_y(-step if way == 0 else step)
                gather_y(way, step - 1, k, source).wait_recv()
                if step < 3 or (step == 3 and k % 2 == way):
                    start(gather_y(way, step, k, source))
        normalize(at_y(step))
        if step < 4:
            normalize(at_y(-step))
        project(completed(step), step - 1)
        if step < 4:
            turn(step)
        if step == 2:
            og_copy.wait()
        if step > 2:
            activate(step - 2)
    activate(3)

    def inner_lo(replica, group):
        piece = inner.at[replica, group]
        return remote(
            piece, piece, lo_send.at[group], inner_recv.at[replica, group], replica=other_lo
        )

    def inner_core(replica, group):
        piece = inner.at[replica, group]
        return remote(
            piece, piece, core_send.at[replica // 2, group], inner_recv.at[replica, group],
            replica=other_core,
        )

    def every(replica):
        return jnp.concatenate([inner[replica, g] for g in range(NX)], axis=1)


    def take_group(step):
        group = completed(step)

        @pl.when(group != x)
        def _():
            for i in range(PARTS):
                inner_x(1, group, i).wait_recv()

        start(inner_lo(r, group))
        start(inner_core(r, group))
        part[:, pl.ds(pl.multiple_of(group * TOK, TOK), TOK)] = jnp.dot(
            w_turned[...], inner[r, group], preferred_element_type=F32
        )

    def part_of(target, k):
        start_row = pl.multiple_of(lax.rem(target, 2) * HALF + at_z(k) * FEAT, FEAT)
        lane = pl.multiple_of(lax.rem(target // 2 + 2, NX) * TOK, TOK)
        return part[pl.ds(start_row, FEAT), pl.ds(lane, TOK)]

    def ring_copy(way, h, k):
        return remote(
            ytx.at[way, h - 1, k],
            yrx.at[way, h - 1, k],
            ys_send.at[way, h - 1, k],
            ys_recv.at[way, h - 1, k],
            mp=mp(at_y(1 - 2 * way), z),
        )

    def ring_send(way, h, k):
        value = part_of(at_y((1 - 2 * way) * h), k)
        if h < (4 if k % 2 == way else 3):
            ring_copy(way, h + 1, k).wait_recv()
            value = value + yrx[way, h, k].astype(F32)
        ytx[way, h - 1, k] = value.astype(BF16)
        start(ring_copy(way, h, k))

    def ring_round(h, ks):
        for k in ks:
            for way in range(2):
                if h < 4 or k % 2 == way:
                    ring_send(way, h, k)

    def rows_of(replica, piece):
        return jnp.concatenate([site_rows[replica, g, piece, :] for g in range(NX)], axis=1)

    def own_rows(piece):
        return jnp.concatenate([normed[2 * g + c, piece, :] for g in range(NX)], axis=1)

    def weight_piece(left, right):
        return lax.dot_general(left, right, (((1,), (1,)), ((), ())), preferred_element_type=F32)

    def wait_rows(replica, features):
        for g in range(NX):
            site_copy(replica, 2 * g, other_core, features).wait_recv()

    def near_piece(k):
        piece = slice(k * CHUNK, (k + 1) * CHUNK)
        w_sum[k] = weight_piece(every(r), own_rows(piece))
        w_sum[k] += weight_piece(every(other_core), rows_of(other_core, piece))

    def sum_copy():
        return remote(lo_tx, lo_rx, sum_send.at[0], sum_recv.at[0], replica=other_lo)

    def wait_inner(replica):
        for g in range(NX):
            inner_core(replica, g).wait_recv()

    def pass_on(step):
        inner_lo(other_lo, completed(step)).wait_recv()
        start(inner_core(other_lo, completed(step)))

    def done_copy(k, half):
        return remote(
            done.at[half, k], done.at[half, k], fin_send.at[k], fin_recv.at[k], replica=other_core
        )

    out_copies = []

    def out_copy(half, k, index):
        copy = pltpu.make_async_copy(
            done.at[half, k],
            wg_hbm.at[:, pl.ds(pl.multiple_of(half * HALF + k * CHUNK, CHUNK), CHUNK)],
            out_sem.at[index, k],
        )
        copy.start()
        out_copies.append(copy)

    order = (1, 3, 2, 0)
    take_group(1)
    ring_round(4, order)
    activate(4)
    take_group(2)
    ring_round(3, order)
    take_group(3)
    ring_round(2, order)
    take_group(4)
    ring_round(1, order)
    def scatter_z(step, source):
        return remote(
            ztx.at[step], zrx.at[source], zs_send.at[step], zs_recv.at[source], mp=mp(y, at_z(step))
        )

    back_copy = remote(
        last_tx, ng_ref, perm_send.at[1], perm_recv.at[1], dp=back_x, mp=mp(y_back, z)
    )

    for k in order:
        for way in range(2):
            ring_copy(way, 1, k).wait_recv()
        total = part_of(y, k) + yrx[0, 0, k].astype(F32) + yrx[1, 0, k].astype(F32)
        if k:
            ztx[k] = total.astype(BF16)
            start(scatter_z(k, z))

    pass_on(1)
    pass_on(2)
    wait_inner(other_core)
    wait_rows(other_core, HALF)
    near_piece(PIECES - 1)
    lo_tx[...] = w_sum[PIECES - 1].astype(BF16)
    start(sum_copy())
    for step in range(1, NZ):
        scatter_z(step, at_z(step)).wait_recv()
        total = total + zrx[at_z(step)].astype(F32)
    last_tx[...] = total.astype(BF16)
    start(back_copy)
    for k in range(FAR):
        near_piece(k)
    pass_on(3)
    pass_on(4)
    wait_rows(other_lo, FAR * CHUNK)
    for k in range(FAR):
        w_far[k] = weight_piece(every(other_lo), rows_of(other_lo, slice(k * CHUNK, (k + 1) * CHUNK)))
    wait_inner(across)
    wait_rows(across, FAR * CHUNK)

    def finish(k, total):
        done[pl.ds(c, 1), k] = (total * 0.25).astype(BF16)[None]
        start(done_copy(k, c))
        out_copy(c, k, 0)

    for k in range(FAR):
        far = w_far[k] + weight_piece(
            every(across), rows_of(across, slice(k * CHUNK, (k + 1) * CHUNK))
        )
        finish(k, w_sum[k] + far)
    sum_copy().wait_recv()
    finish(PIECES - 1, lo_tx[...].astype(F32) + lo_rx[...].astype(F32))
    for k in range(PIECES):
        done_copy(k, 1 - c).wait_recv()
        out_copy(1 - c, k, 1)

    @pl.when(moves)
    def _():
        perm_copy().wait_send()


    for index in range(NX):
        @pl.when(completed(index + 1) != x)
        def _(index=index):
            for i in range(PARTS):
                proj_copy(completed(index + 1), index, i).wait_send()

    for g in range(NX):
        site_copy(r, 2 * g + 1 - c, other_core, HALF).wait_send()
    for step in range(1, NX):
        for i in range(PARTS):
            inner_x(step, x, i).wait_send()
    back_copy.wait_recv()
    for copy in copies:
        copy.wait_send()
    for copy in out_copies:
        copy.wait()


def hand_over(act_in, ng_in, wg_in, act_out, ng_out, wg_out, act, ng, wg, sem):
    pieces = [(act_in, act, act_out), (ng_in, ng, ng_out)]
    for i in range(6):
        piece = pl.ds(i * 112, 112)
        pieces.append((wg_in.at[piece, :], wg.at[piece, :], wg_out.at[piece, :]))
    loads = [
        pltpu.make_async_copy(source, held, sem.at[0, i]) for i, (source, held, _) in enumerate(pieces)
    ]
    stores = [
        pltpu.make_async_copy(held, target, sem.at[1, i]) for i, (_, held, target) in enumerate(pieces)
    ]
    for load in loads:
        load.start()
    for load, store in zip(loads, stores):
        load.wait()
        store.start()
    for store in stores:
        store.wait()


def local(tokens, norm_gain, joined_weight, output_grad):
    vmem = pl.BlockSpec(memory_space=pltpu.VMEM)
    anywhere = pl.BlockSpec(memory_space=pl.ANY)
    dma = pltpu.SemaphoreType.DMA
    scratch = [
        pltpu.VMEM((COLS, 2 * HALF), BF16),
        pltpu.VMEM((2 * HALF, COLS), BF16),
        pltpu.VMEM((COLS, TOK), BF16),
        pltpu.VMEM((D // 128, 128), F32),
        pltpu.VMEM((2 * HALF, TOK), F32),
        pltpu.VMEM((8, 128), F32),
        pltpu.VMEM((8, 128), F32),
        pltpu.VMEM((NZ, 8, 128), F32),
        pltpu.VMEM((NY, 8, 128), F32),
        pltpu.VMEM((NX, 8, 128), F32),
        pltpu.VMEM((NY, HALF, TOK), BF16),
        pltpu.VMEM((NY, HALF, TOK), BF16),
        pltpu.VMEM((4, NX, HALF, TOK), BF16),
        pltpu.VMEM((NX, COLS, TOK), BF16),
        pltpu.VMEM((NX, COLS, TOK), BF16),
        pltpu.VMEM((COLS, TOK), F32),
        pltpu.VMEM((4, NX, COLS, TOK), BF16),
        pltpu.VMEM((2 * HALF, NX * TOK), F32),
        pltpu.VMEM((2, 4, NZ, FEAT, TOK), BF16),
        pltpu.VMEM((2, 4, NZ, FEAT, TOK), BF16),
        pltpu.VMEM((NZ, FEAT, TOK), BF16),
        pltpu.VMEM((NZ, FEAT, TOK), BF16),
        pltpu.VMEM((FEAT, TOK), BF16),
        pltpu.VMEM((PIECES, COLS, CHUNK), F32),
        pltpu.VMEM((FAR, COLS, CHUNK), F32),
        pltpu.VMEM((COLS, CHUNK), BF16),
        pltpu.VMEM((COLS, CHUNK), BF16),
        pltpu.VMEM((2, PIECES, COLS, CHUNK), BF16),
        dma((2,)),
        dma((2, PIECES)),
        dma((NZ + NY + NX,)),
        dma((NZ + NY + NX,)),
        dma((2,)),
        dma((2,)),
        dma((NZ,)),
        dma((NZ,)),
        dma((2, 4, NZ)),
        dma((2, 4, NZ)),
        dma((2, NY)),
        dma((4, NX)),
        dma((NX, PARTS)),
        dma((NX, PARTS)),
        dma((NX, PARTS)),
        dma((NX, PARTS)),
        dma((NX,)),
        dma((2, NX)),
        dma((4, NX)),
        dma((2, 4, NZ)),
        dma((2, 4, NZ)),
        dma((NZ,)),
        dma((NZ,)),
        dma((1,)),
        dma((1,)),
        dma((PIECES,)),
        dma((PIECES,)),
    ]
    shapes = (
        jax.ShapeDtypeStruct((COLS, TOK), BF16),
        jax.ShapeDtypeStruct((FEAT, TOK), BF16),
        jax.ShapeDtypeStruct((COLS, 2 * HALF), BF16),
    )
    results = pl.pallas_call(
        kernel,
        out_shape=shapes,
        in_specs=[vmem, vmem, anywhere, anywhere],
        out_specs=(vmem, vmem, anywhere),
        scratch_shapes=scratch,
        compiler_params=pltpu.CompilerParams(
            collective_id=0, has_side_effects=True, vmem_limit_bytes=56 * 1024 * 1024
        ),
        cost_estimate=pl.CostEstimate(flops=3200000000, bytes_accessed=5000000, transcendentals=200000),
    )(
        tokens.T,
        norm_gain.reshape(D // 128, 128),
        output_grad.T,
        joined_weight.T,
    )
    activated, normed_grad, weight_grad = pl.pallas_call(
        hand_over,
        out_shape=shapes,
        in_specs=[anywhere] * 3,
        out_specs=(anywhere,) * 3,
        scratch_shapes=[pltpu.VMEM(shape.shape, BF16) for shape in shapes] + [dma((2, 8))],
        cost_estimate=pl.CostEstimate(flops=0, bytes_accessed=4600000, transcendentals=0),
    )(*results)
    return activated.T, normed_grad.T, weight_grad.T


def solution(mesh):
    in_specs = (P(("replica", "dp"), "mp"), P(), P("dp", "mp"), P(("replica", "dp"), "mp"))
    out_specs = (P(("replica", "dp"), "mp"), P(("replica", "dp"), "mp"), P("dp", "mp"))
    return jax.shard_map(local, mesh=mesh, in_specs=in_specs, out_specs=out_specs, check_vma=False)
```

```python
import jax
import jax.numpy as jnp
from jax import lax
from jax.experimental import pallas as pl
from jax.experimental.pallas import tpu as pltpu
from jax.sharding import PartitionSpec as P

MESH = pl.DeviceIdType.MESH
F32 = jnp.float32
BF16 = jnp.bfloat16

NX = 4
NY = 8
NZ = 4
TOK = 128
FEAT = 192
HALF = NZ * FEAT
COLS = 672
QKV = 288
D = 6144
CHUNK = 256
PIECES = HALF // CHUNK
FAR = 2
PIECE = 176
PADDED = NX * PIECE


def remote(src, dst, send_sem, recv_sem, **device):
    return pltpu.make_async_remote_copy(
        src_ref=src,
        dst_ref=dst,
        send_sem=send_sem,
        recv_sem=recv_sem,
        device_id=device,
        device_id_type=MESH,
    )


def merge_stats(stack, features):
    count = stack.shape[0]
    means = stack[:, 0:1, :]
    mean = jnp.sum(means, axis=0) / count
    squares = jnp.sum(stack[:, 1:2, :], axis=0) + features * jnp.sum(
        jnp.square(means - mean[None]), axis=0
    )
    return stats_table(mean, squares)


def stats_table(mean, squares):
    row = lax.broadcasted_iota(jnp.int32, (8, 128), 0)
    return jnp.where(row == 0, mean, jnp.where(row == 1, squares, 0.0))


def kernel(
    tok_hbm, gain_hbm, og_hbm, w_hbm, act_ref, ng_ref, wg_hbm,
    tok_ref, gain_ref, w, w_turned, og, og_rx, gain_rows, gain, stat_z_tx, stat_y_tx, stat_z, stat_y, stat_x, rows, normed,
    site_rows, proj_tx, proj_rx, proj_own, act_tx, act_all, inner, part, ytx, yrx, ztx, zrx, last_tx,
    w_sum, w_far, lo_tx, lo_rx, done,
    w_sem, out_sem, stat_send, stat_recv, perm_send, perm_recv, zg_send, zg_recv,
    yg_send, yg_recv, site_send, site_recv, og_send, og_recv, px_send, px_recv, ix_send, ix_recv, act_send, act_recv, lo_send, core_send, inner_recv,
    ys_send, ys_recv, zs_send, zs_recv, sum_send, sum_recv, fin_send, fin_recv,
):
    r = lax.axis_index("replica")
    x = lax.axis_index("dp")
    m = lax.axis_index("mp")
    y = m // NZ
    z = lax.rem(m, NZ)
    a = y // 2
    b = lax.rem(y, 2)
    y_back = 2 * x + b
    back_x = lax.rem(a + 2, NX)
    from_y = 2 * lax.rem(x + 2, NX) + b
    c = lax.rem(r, 2)
    other_core = r + 1 - 2 * c
    other_lo = lax.rem(r + 2, 4)
    across = 3 - r
    moves = a != x

    def at_z(step):
        return lax.rem(z + step, NZ)

    def at_y(step):
        return lax.rem(y + step + NY, NY)

    def at_x(step):
        return lax.rem(x + step, NX)

    def mp(y_place, z_place):
        return y_place * NZ + z_place

    copies = []

    def start(copy):
        copies.append(copy)
        copy.start()

    tok_copy = pltpu.make_async_copy(tok_hbm, tok_ref, w_sem.at[2])
    gain_copy = pltpu.make_async_copy(gain_hbm, gain_ref, w_sem.at[3])
    tok_copy.start()
    gain_copy.start()

    barrier = pltpu.get_barrier_semaphore()
    greeted = [{"mp": mp(y, at_z(step))} for step in range(1, NZ)]
    greeted += [{"mp": mp(at_y(step), z)} for step in range(1, NY)]
    greeted += [{"dp": at_x(step)} for step in range(1, NX)]
    greeted += [{"replica": other_core}, {"replica": other_lo}, {"replica": across}]
    greeted += [{"dp": a, "mp": mp(from_y, z)}]
    for device in greeted:
        pl.semaphore_signal(barrier, inc=1, device_id=device, device_id_type=MESH)

    @pl.when(moves)
    def _():
        pl.semaphore_signal(
            barrier, inc=1, device_id={"dp": a, "mp": mp(y_back, z)}, device_id_type=MESH
        )

    w_copy = pltpu.make_async_copy(w_hbm, w, w_sem.at[0])
    og_copy = pltpu.make_async_copy(og_hbm, og.at[pl.ds(0, COLS), :], w_sem.at[1])
    w_copy.start()
    og_copy.start()

    tok_copy.wait()
    values = tok_ref[...].astype(F32)
    mean = jnp.mean(values, axis=0, keepdims=True)
    squares = jnp.sum(jnp.square(values - mean), axis=0, keepdims=True)
    stats = stats_table(mean, squares)
    stat_z_tx[...] = stats
    stat_z[pl.ds(z, 1)] = stats[None]

    pl.semaphore_wait(barrier, len(greeted) + jnp.where(moves, 1, 0))

    def z_block(source_y, source_z):
        return rows.at[source_y, pl.ds(pl.multiple_of(source_z * FEAT, FEAT), FEAT), :]

    def perm_copy():
        return remote(
            tok_ref, z_block(y_back, z), perm_send.at[0], perm_recv.at[0], dp=a, mp=mp(y_back, z)
        )

    def stat_z_copy(step, slot):
        return remote(
            stat_z_tx, stat_z.at[slot], stat_send.at[step], stat_recv.at[slot], mp=mp(y, at_z(step))
        )

    def stat_y_copy(step, slot):
        return remote(
            stat_y_tx, stat_y.at[slot], stat_send.at[NZ + step], stat_recv.at[NZ + slot],
            mp=mp(at_y(step), z),
        )

    def stat_x_copy(step, slot):
        return remote(
            stat_x.at[slot], stat_x.at[slot], stat_send.at[NZ + NY + step],
            stat_recv.at[NZ + NY + slot], dp=at_x(step),
        )

    @pl.when(moves)
    def _():
        perm_copy().start()

    for step in range(1, NZ):
        start(stat_z_copy(step, z))

    @pl.when(jnp.logical_not(moves))
    def _():
        rows[pl.ds(y, 1), pl.ds(pl.multiple_of(z * FEAT, FEAT), FEAT), :] = tok_ref[...][None]

    def quarter(place):
        return pl.ds(pl.multiple_of(place * PIECE, 16), PIECE)

    def og_spread(step, source):
        return remote(
            og.at[quarter(at_x(step)), :], og_rx.at[source], og_send.at[step], og_recv.at[source],
            dp=at_x(step),
        )

    nothing = jnp.zeros((PADDED - COLS, TOK), F32)
    og[COLS:, :] = nothing.astype(BF16)
    for index in range(NX):
        proj_own[index, COLS:, :] = nothing
        proj_tx[index, COLS:, :] = nothing.astype(BF16)
    og_copy.wait()
    og_rx[pl.ds(x, 1)] = og[quarter(x), :][None]
    for step in range(1, NX):
        start(og_spread(step, x))

    def turn(piece):
        columns = slice(piece * HALF // 2, (piece + 1) * HALF // 2)
        w_turned[columns, :] = jnp.transpose(w[:, columns])

    gain_copy.wait()
    gain_rows[...] = gain_ref[...].astype(F32)
    table = jnp.transpose(
        jnp.concatenate([gain_rows[pl.ds(12 * x, 12), :], jnp.zeros((116, 128), F32)], axis=0)
    )
    for i in range(12):
        gain[i * 128 : (i + 1) * 128, :] = jnp.broadcast_to(table[:, i : i + 1], (128, 128))

    for step in range(1, NZ):
        stat_z_copy(step, at_z(step)).wait_recv()
    stats = merge_stats(stat_z[...], float(FEAT))
    stat_y_tx[...] = stats
    stat_y[pl.ds(y, 1)] = stats[None]
    for step in range(1, NY):
        start(stat_y_copy(step, y))
    w_copy.wait()
    turn(0)
    turn(1)

    @pl.when(moves)
    def _():
        perm_copy().wait_recv()


    def gather_z(step, source):
        piece = z_block(y, source)
        return remote(piece, piece, zg_send.at[step], zg_recv.at[source], mp=mp(y, at_z(step)))

    def gather_y(way, step, k, source):
        piece = z_block(source, at_z(k))
        return remote(
            piece, piece, yg_send.at[way, step, k], yg_recv.at[way, step, k],
            mp=mp(at_y(1 - 2 * way), z),
        )

    for step in range(1, NZ):
        start(gather_z(step, z))
    for way in range(2):
        start(gather_y(way, 0, 0, y))
    turn(2)
    for step in range(1, NY):
        stat_y_copy(step, at_y(step)).wait_recv()
    stat_x[pl.ds(x, 1)] = merge_stats(stat_y[...], float(HALF))[None]
    for step in range(1, NX):
        start(stat_x_copy(step, x))
    turn(3)

    def receive(step, k):
        for way in range(2):
            if step < 4 or k % 2 == way:
                source = at_y(-step if way == 0 else step)
                gather_y(way, step - 1, k, source).wait_recv()
                if step < 3 or (step == 3 and k % 2 == way):
                    start(gather_y(way, step, k, source))

    arrivals = (0, 1, 3, 2)
    receive(1, 0)
    for k in arrivals[1:]:
        gather_z(k, at_z(k)).wait_recv()
        for way in range(2):
            start(gather_y(way, 0, k, y))
    def site_copy(source, t, replica, features):
        piece = pl.ds(0, features)
        return remote(
            normed.at[t, piece, :], site_rows.at[source, t // 2, piece, :],
            site_send.at[replica // 2, t], site_recv.at[source, t // 2], replica=replica,
        )

    def normalize(t):
        h = lax.rem(t, 2)
        statistics = stat_x[t // 2]
        scale = lax.rsqrt(statistics[1:2] * (1.0 / D) + 1e-06)
        column = gain[pl.ds(pl.multiple_of(h * HALF, HALF), HALF), :]
        value = (rows[t].astype(F32) - statistics[0:1]) * scale * column
        normed[pl.ds(t, 1)] = value.astype(BF16)[None]
        start(site_copy(r, t, 2 * (1 - r // 2) + h, FAR * CHUNK))

        @pl.when(h != c)
        def _():
            site_copy(r, t, other_core, HALF).start()

    def project(step, low, high):
        group = completed(step)
        total = jnp.dot(
            w[low:high, :HALF], normed[2 * group], preferred_element_type=F32
        ) + jnp.dot(w[low:high, HALF:], normed[2 * group + 1], preferred_element_type=F32)
        proj_own[step - 1, low:high, :] = total
        proj_tx[step - 1, low:high, :] = total.astype(BF16)

    def proj_copy(step, other, source):
        return remote(
            proj_tx.at[step - 1, quarter(at_x(other)), :], proj_rx.at[step - 1, source],
            px_send.at[step - 1, other], px_recv.at[step - 1, source], dp=at_x(other),
        )

    def spread(step):
        for other in range(1, NX):
            start(proj_copy(step, other, x))

    def inner_x(step, other, source):
        piece = inner.at[r, completed(step), quarter(source), :]
        return remote(
            piece, piece, ix_send.at[step - 1, other], ix_recv.at[step - 1, source], dp=at_x(other)
        )

    def act_copy(step, source, to):
        return remote(
            act_tx.at[step - 1], act_all.at[quarter(source), :],
            act_send.at[step - 1], act_recv.at[source], dp=to,
        )

    def activate(step):
        group = completed(step)
        for other in range(1, NX):
            proj_copy(step, other, at_x(other)).wait_recv()
        projected = proj_own[step - 1, quarter(x), :]
        for other in range(1, NX):
            projected = projected + proj_rx[step - 1, at_x(other)].astype(F32)
        linear = lax.broadcasted_iota(jnp.int32, (PIECE, TOK), 0) + x * PIECE < QKV
        normal_cdf = 0.5 * (1.0 + lax.erf(projected * 0.7071067811865476))
        density = jnp.exp(-0.5 * projected * projected) * 0.3989422804014327
        slopes = jnp.where(linear, 1.0, normal_cdf + projected * density)
        inner[pl.ds(r, 1), pl.ds(group, 1), quarter(x), :] = (
            og_rx[group].astype(F32) * slopes
        ).astype(BF16)[None, None]
        for other in range(1, NX):
            start(inner_x(step, other, x))
        act_tx[step - 1] = jnp.where(linear, projected, projected * normal_cdf).astype(BF16)

        @pl.when(group != x)
        def _():
            act_copy(step, x, group).start()

        @pl.when(group == x)
        def _():
            act_all[quarter(x), :] = act_tx[step - 1]

    sign = 1 - 2 * b

    def completed(step):
        return at_y(step * sign if step % 2 else -step * sign) // 2

    def own_row():
        for step in range(1, NX):
            stat_x_copy(step, at_x(step)).wait_recv()
        normalize(y)

    def tasks(step):
        yield lambda: normalize(at_y(step))
        if step < 4:
            yield lambda: normalize(at_y(-step))
        yield lambda: project(step, 0, COLS // 2)
        yield lambda: (project(step, COLS // 2, COLS), spread(step))
        if step == 2:
            yield wait_og
        if 1 < step < 4:
            yield lambda: activate(step - 1)

    def wait_og():
        for other in range(1, NX):
            og_spread(other, at_x(other)).wait_recv()

    receive(1, 1)
    own_row()
    receive(1, 3)
    receive(1, 2)
    for step in range(1, 5):
        work = list(tasks(step))
        if step < 4:
            for k in arrivals:
                for task in work[:2]:
                    task()
                work = work[2:]
                receive(step + 1, k)
        for task in work:
            task()

    def inner_lo(replica, group):
        piece = inner.at[replica, group, pl.ds(0, COLS), :]
        return remote(
            piece, piece, lo_send.at[group], inner_recv.at[replica, group], replica=other_lo
        )

    def inner_core(replica, group):
        piece = inner.at[replica, group, pl.ds(0, COLS), :]
        return remote(
            piece, piece, core_send.at[replica // 2, group], inner_recv.at[replica, group],
            replica=other_core,
        )

    def take_group(step):
        group = completed(step)
        for other in range(1, NX):
            inner_x(step, other, at_x(other)).wait_recv()
        start(inner_lo(r, group))
        start(inner_core(r, group))
        part[:, pl.ds(pl.multiple_of(group * TOK, TOK), TOK)] = jnp.dot(
            w_turned[...], inner[r, group, 0:COLS, :], preferred_element_type=F32
        )

    def part_of(target, k):
        start_row = pl.multiple_of(lax.rem(target, 2) * HALF + at_z(k) * FEAT, FEAT)
        lane = pl.multiple_of(lax.rem(target // 2 + 2, NX) * TOK, TOK)
        return part[pl.ds(start_row, FEAT), pl.ds(lane, TOK)]

    def ring_copy(way, h, k):
        return remote(
            ytx.at[way, h - 1, k],
            yrx.at[way, h - 1, k],
            ys_send.at[way, h - 1, k],
            ys_recv.at[way, h - 1, k],
            mp=mp(at_y(1 - 2 * way), z),
        )

    def ring_send(way, h, k):
        value = part_of(at_y((1 - 2 * way) * h), k)
        if h < (4 if k % 2 == way else 3):
            ring_copy(way, h + 1, k).wait_recv()
            value = value + yrx[way, h, k].astype(F32)
        ytx[way, h - 1, k] = value.astype(BF16)
        start(ring_copy(way, h, k))

    def ring_round(h, ks):
        for k in ks:
            for way in range(2):
                if h < 4 or k % 2 == way:
                    ring_send(way, h, k)

    def wait_rows(replica, features):
        for g in range(NX):
            site_copy(replica, 2 * g, other_core, features).wait_recv()

    def weight_piece(left, right):
        return lax.dot_general(left, right, (((1,), (1,)), ((), ())), preferred_element_type=F32)

    def add_near(step):
        g = completed(step)
        inner_core(other_core, g).wait_recv()
        left = jnp.concatenate([inner[r, g, 0:COLS, :], inner[other_core, g, 0:COLS, :]], axis=1)
        for k in reversed(range(PIECES)):
            piece = slice(k * CHUNK, (k + 1) * CHUNK)
            right = jnp.concatenate(
                [normed[2 * g + c, piece, :], site_rows[other_core, g, piece, :]], axis=1
            )
            w_sum[k] = weight_piece(left, right) + (w_sum[k] if step > 1 else 0.0)

    def far_piece(step, k):
        g = completed(step)
        left = jnp.concatenate([inner[other_lo, g, 0:COLS, :], inner[across, g, 0:COLS, :]], axis=1)
        piece = slice(k * CHUNK, (k + 1) * CHUNK)
        right = jnp.concatenate(
            [site_rows[other_lo, g, piece, :], site_rows[across, g, piece, :]], axis=1
        )
        return weight_piece(left, right) + (w_far[k] if step > 1 else 0.0)

    def add_far(step):
        inner_core(across, completed(step)).wait_recv()
        for k in range(FAR):
            w_far[k] = far_piece(step, k)

    def sum_copy():
        return remote(lo_tx, lo_rx, sum_send.at[0], sum_recv.at[0], replica=other_lo)

    def pass_on(step):
        inner_lo(other_lo, completed(step)).wait_recv()
        start(inner_core(other_lo, completed(step)))

    def done_copy(k, half):
        return remote(
            done.at[half, k], done.at[half, k], fin_send.at[k], fin_recv.at[k], replica=other_core
        )

    out_copies = []

    def out_copy(half, k, index):
        copy = pltpu.make_async_copy(
            done.at[half, k],
            wg_hbm.at[:, pl.ds(pl.multiple_of(half * HALF + k * CHUNK, CHUNK), CHUNK)],
            out_sem.at[index, k],
        )
        copy.start()
        out_copies.append(copy)

    order = (1, 3, 2, 0)
    take_group(1)
    ring_round(4, order)
    activate(3)
    take_group(2)
    ring_round(3, order)
    activate(4)
    take_group(3)
    ring_round(2, order)
    wait_rows(other_core, HALF)
    add_near(1)
    add_near(2)
    take_group(4)
    ring_round(1, order)
    def scatter_z(step, source):
        return remote(
            ztx.at[step], zrx.at[source], zs_send.at[step], zs_recv.at[source], mp=mp(y, at_z(step))
        )

    back_copy = remote(
        last_tx, ng_ref, perm_send.at[1], perm_recv.at[1], dp=back_x, mp=mp(y_back, z)
    )

    for k in order:
        for way in range(2):
            ring_copy(way, 1, k).wait_recv()
        total = part_of(y, k) + yrx[0, 0, k].astype(F32) + yrx[1, 0, k].astype(F32)
        if k:
            ztx[k] = total.astype(BF16)
            start(scatter_z(k, z))

    add_near(3)
    add_near(4)
    lo_tx[...] = w_sum[PIECES - 1].astype(BF16)
    start(sum_copy())
    pass_on(1)
    pass_on(2)
    pass_on(3)
    for step in range(1, NZ):
        scatter_z(step, at_z(step)).wait_recv()
        total = total + zrx[at_z(step)].astype(F32)
    last_tx[...] = total.astype(BF16)
    start(back_copy)
    wait_rows(other_lo, FAR * CHUNK)
    wait_rows(across, FAR * CHUNK)
    add_far(1)
    add_far(2)
    pass_on(4)
    add_far(3)

    def finish(k, total):
        done[pl.ds(c, 1), k] = (total * 0.25).astype(BF16)[None]
        start(done_copy(k, c))
        out_copy(c, k, 0)

    inner_core(across, completed(4)).wait_recv()
    for k in range(FAR):
        finish(k, w_sum[k] + far_piece(4, k))
    sum_copy().wait_recv()
    finish(PIECES - 1, lo_tx[...].astype(F32) + lo_rx[...].astype(F32))
    for k in range(PIECES):
        done_copy(k, 1 - c).wait_recv()
        out_copy(1 - c, k, 1)

    for other in range(1, NX):
        act_copy(1, at_x(other), at_x(other)).wait_recv()
    act_ref[...] = act_all[0:COLS, :]

    @pl.when(moves)
    def _():
        perm_copy().wait_send()


    for step in range(1, 5):
        @pl.when(completed(step) != x)
        def _(step=step):
            act_copy(step, x, completed(step)).wait_send()

    for g in range(NX):
        site_copy(r, 2 * g + 1 - c, other_core, HALF).wait_send()
    back_copy.wait_recv()
    for copy in copies:
        copy.wait_send()
    for copy in out_copies:
        copy.wait()


def hand_over(act_in, ng_in, wg_in, act_out, ng_out, wg_out, act, ng, wg, sem):
    pieces = [(act_in, act, act_out), (ng_in, ng, ng_out)]
    for i in range(6):
        piece = pl.ds(i * 112, 112)
        pieces.append((wg_in.at[piece, :], wg.at[piece, :], wg_out.at[piece, :]))
    loads = [
        pltpu.make_async_copy(source, held, sem.at[0, i]) for i, (source, held, _) in enumerate(pieces)
    ]
    stores = [
        pltpu.make_async_copy(held, target, sem.at[1, i]) for i, (_, held, target) in enumerate(pieces)
    ]
    for load in loads:
        load.start()
    for load, store in zip(loads, stores):
        load.wait()
        store.start()
    for store in stores:
        store.wait()


def local(tokens, norm_gain, joined_weight, output_grad):
    vmem = pl.BlockSpec(memory_space=pltpu.VMEM)
    anywhere = pl.BlockSpec(memory_space=pl.ANY)
    dma = pltpu.SemaphoreType.DMA
    scratch = [
        pltpu.VMEM((FEAT, TOK), BF16),
        pltpu.VMEM((D // 128, 128), BF16),
        pltpu.VMEM((COLS, 2 * HALF), BF16),
        pltpu.VMEM((2 * HALF, COLS), BF16),
        pltpu.VMEM((PADDED, TOK), BF16),
        pltpu.VMEM((NX, PIECE, TOK), BF16),
        pltpu.VMEM((D // 128, 128), F32),
        pltpu.VMEM((2 * HALF, TOK), F32),
        pltpu.VMEM((8, 128), F32),
        pltpu.VMEM((8, 128), F32),
        pltpu.VMEM((NZ, 8, 128), F32),
        pltpu.VMEM((NY, 8, 128), F32),
        pltpu.VMEM((NX, 8, 128), F32),
        pltpu.VMEM((NY, HALF, TOK), BF16),
        pltpu.VMEM((NY, HALF, TOK), BF16),
        pltpu.VMEM((4, NX, HALF, TOK), BF16),
        pltpu.VMEM((NX, PADDED, TOK), BF16),
        pltpu.VMEM((NX, NX, PIECE, TOK), BF16),
        pltpu.VMEM((NX, PADDED, TOK), F32),
        pltpu.VMEM((NX, PIECE, TOK), BF16),
        pltpu.VMEM((PADDED, TOK), BF16),
        pltpu.VMEM((4, NX, PADDED, TOK), BF16),
        pltpu.VMEM((2 * HALF, NX * TOK), F32),
        pltpu.VMEM((2, 4, NZ, FEAT, TOK), BF16),
        pltpu.VMEM((2, 4, NZ, FEAT, TOK), BF16),
        pltpu.VMEM((NZ, FEAT, TOK), BF16),
        pltpu.VMEM((NZ, FEAT, TOK), BF16),
        pltpu.VMEM((FEAT, TOK), BF16),
        pltpu.VMEM((PIECES, COLS, CHUNK), F32),
        pltpu.VMEM((FAR, COLS, CHUNK), F32),
        pltpu.VMEM((COLS, CHUNK), BF16),
        pltpu.VMEM((COLS, CHUNK), BF16),
        pltpu.VMEM((2, PIECES, COLS, CHUNK), BF16),
        dma((4,)),
        dma((2, PIECES)),
        dma((NZ + NY + NX,)),
        dma((NZ + NY + NX,)),
        dma((2,)),
        dma((2,)),
        dma((NZ,)),
        dma((NZ,)),
        dma((2, 4, NZ)),
        dma((2, 4, NZ)),
        dma((2, NY)),
        dma((4, NX)),
        dma((NX,)),
        dma((NX,)),
        dma((NX, NX)),
        dma((NX, NX)),
        dma((NX, NX)),
        dma((NX, NX)),
        dma((NX,)),
        dma((NX,)),
        dma((NX,)),
        dma((2, NX)),
        dma((4, NX)),
        dma((2, 4, NZ)),
        dma((2, 4, NZ)),
        dma((NZ,)),
        dma((NZ,)),
        dma((1,)),
        dma((1,)),
        dma((PIECES,)),
        dma((PIECES,)),
    ]
    shapes = (
        jax.ShapeDtypeStruct((COLS, TOK), BF16),
        jax.ShapeDtypeStruct((FEAT, TOK), BF16),
        jax.ShapeDtypeStruct((COLS, 2 * HALF), BF16),
    )
    results = pl.pallas_call(
        kernel,
        out_shape=shapes,
        in_specs=[anywhere] * 4,
        out_specs=(vmem, vmem, anywhere),
        scratch_shapes=scratch,
        compiler_params=pltpu.CompilerParams(
            collective_id=0, has_side_effects=True, vmem_limit_bytes=56 * 1024 * 1024
        ),
        cost_estimate=pl.CostEstimate(flops=3200000000, bytes_accessed=5000000, transcendentals=200000),
    )(
        tokens.T,
        norm_gain.reshape(D // 128, 128),
        output_grad.T,
        joined_weight.T,
    )
    activated, normed_grad, weight_grad = pl.pallas_call(
        hand_over,
        out_shape=shapes,
        in_specs=[anywhere] * 3,
        out_specs=(anywhere,) * 3,
        scratch_shapes=[pltpu.VMEM(shape.shape, BF16) for shape in shapes] + [dma((2, 8))],
        cost_estimate=pl.CostEstimate(flops=0, bytes_accessed=4600000, transcendentals=0),
    )(*results)
    return activated.T, normed_grad.T, weight_grad.T


def solution(mesh):
    in_specs = (P(("replica", "dp"), "mp"), P(), P("dp", "mp"), P(("replica", "dp"), "mp"))
    out_specs = (P(("replica", "dp"), "mp"), P(("replica", "dp"), "mp"), P("dp", "mp"))
    return jax.shard_map(local, mesh=mesh, in_specs=in_specs, out_specs=out_specs, check_vma=False)
```

```python
import jax
import jax.numpy as jnp
from jax import lax
from jax.experimental import pallas as pl
from jax.experimental.pallas import tpu as pltpu
from jax.sharding import PartitionSpec as P

MESH = pl.DeviceIdType.MESH
F32 = jnp.float32
BF16 = jnp.bfloat16

NX = 4
NY = 8
NZ = 4
TOK = 128
FEAT = 192
HALF = NZ * FEAT
COLS = 672
QKV = 288
D = 6144
CHUNK = 256
PIECES = HALF // CHUNK
FAR = 2
PIECE = 176
PADDED = NX * PIECE


def remote(src, dst, send_sem, recv_sem, **device):
    return pltpu.make_async_remote_copy(
        src_ref=src,
        dst_ref=dst,
        send_sem=send_sem,
        recv_sem=recv_sem,
        device_id=device,
        device_id_type=MESH,
    )


def merge_stats(stack, features):
    count = stack.shape[0]
    means = stack[:, 0:1, :]
    mean = jnp.sum(means, axis=0) / count
    squares = jnp.sum(stack[:, 1:2, :], axis=0) + features * jnp.sum(
        jnp.square(means - mean[None]), axis=0
    )
    return stats_table(mean, squares)


def stats_table(mean, squares):
    row = lax.broadcasted_iota(jnp.int32, (8, 128), 0)
    return jnp.where(row == 0, mean, jnp.where(row == 1, squares, 0.0))


def kernel(
    tok_hbm, gain_hbm, og_hbm, w_hbm, act_ref, ng_ref, wg_hbm,
    tok_ref, gain_ref, w, w_turned, og, og_rx, gain_rows, gain, stat_z_tx, stat_y_tx, stat_z, stat_y, stat_x, site_stat, rows, normed,
    site_rows, proj_tx, proj_rx, proj_own, act_tx, act_all, inner, part, ytx, yrx, ztx, zrx, last_tx,
    w_sum, w_far, lo_tx, lo_rx, done,
    w_sem, out_sem, stat_send, stat_recv, perm_send, perm_recv, zg_send, zg_recv,
    yg_send, yg_recv, site_send, site_recv, site_stat_send, site_stat_recv, og_send, og_recv, px_send, px_recv, ix_send, ix_recv, act_send, act_recv, lo_send, core_send, inner_recv,
    ys_send, ys_recv, zs_send, zs_recv, sum_send, sum_recv, fin_send, fin_recv,
):
    r = lax.axis_index("replica")
    x = lax.axis_index("dp")
    m = lax.axis_index("mp")
    y = m // NZ
    z = lax.rem(m, NZ)
    a = y // 2
    b = lax.rem(y, 2)
    y_back = 2 * x + b
    back_x = lax.rem(a + 2, NX)
    from_y = 2 * lax.rem(x + 2, NX) + b
    c = lax.rem(r, 2)
    other_core = r + 1 - 2 * c
    other_lo = lax.rem(r + 2, 4)
    across = 3 - r
    moves = a != x

    def at_z(step):
        return lax.rem(z + step, NZ)

    def at_y(step):
        return lax.rem(y + step + NY, NY)

    def at_x(step):
        return lax.rem(x + step, NX)

    def mp(y_place, z_place):
        return y_place * NZ + z_place

    copies = []

    def start(copy):
        copies.append(copy)
        copy.start()

    tok_copy = pltpu.make_async_copy(tok_hbm, tok_ref, w_sem.at[2])
    gain_copy = pltpu.make_async_copy(gain_hbm, gain_ref, w_sem.at[3])
    tok_copy.start()
    gain_copy.start()

    barrier = pltpu.get_barrier_semaphore()
    greeted = [{"mp": mp(y, at_z(step))} for step in range(1, NZ)]
    greeted += [{"mp": mp(at_y(step), z)} for step in range(1, NY)]
    greeted += [{"dp": at_x(step)} for step in range(1, NX)]
    greeted += [{"replica": other_core}, {"replica": other_lo}, {"replica": across}]
    greeted += [{"dp": a, "mp": mp(from_y, z)}]
    for device in greeted:
        pl.semaphore_signal(barrier, inc=1, device_id=device, device_id_type=MESH)

    @pl.when(moves)
    def _():
        pl.semaphore_signal(
            barrier, inc=1, device_id={"dp": a, "mp": mp(y_back, z)}, device_id_type=MESH
        )

    w_copy = pltpu.make_async_copy(w_hbm, w, w_sem.at[0])
    og_copy = pltpu.make_async_copy(og_hbm, og.at[pl.ds(0, COLS), :], w_sem.at[1])
    w_copy.start()
    og_copy.start()

    tok_copy.wait()
    values = tok_ref[...].astype(F32)
    mean = jnp.mean(values, axis=0, keepdims=True)
    squares = jnp.sum(jnp.square(values - mean), axis=0, keepdims=True)
    stats = stats_table(mean, squares)
    stat_z_tx[...] = stats
    stat_z[pl.ds(z, 1)] = stats[None]

    pl.semaphore_wait(barrier, len(greeted) + jnp.where(moves, 1, 0))

    def z_block(source_y, source_z):
        return rows.at[source_y, pl.ds(pl.multiple_of(source_z * FEAT, FEAT), FEAT), :]

    def perm_copy():
        return remote(
            tok_ref, z_block(y_back, z), perm_send.at[0], perm_recv.at[0], dp=a, mp=mp(y_back, z)
        )

    def stat_z_copy(step, slot):
        return remote(
            stat_z_tx, stat_z.at[slot], stat_send.at[step], stat_recv.at[slot], mp=mp(y, at_z(step))
        )

    def stat_y_copy(step, slot):
        return remote(
            stat_y_tx, stat_y.at[slot], stat_send.at[NZ + step], stat_recv.at[NZ + slot],
            mp=mp(at_y(step), z),
        )

    def stat_x_copy(step, slot):
        return remote(
            stat_x.at[slot], stat_x.at[slot], stat_send.at[NZ + NY + step],
            stat_recv.at[NZ + NY + slot], dp=at_x(step),
        )

    @pl.when(moves)
    def _():
        perm_copy().start()

    for step in range(1, NZ):
        start(stat_z_copy(step, z))

    @pl.when(jnp.logical_not(moves))
    def _():
        rows[pl.ds(y, 1), pl.ds(pl.multiple_of(z * FEAT, FEAT), FEAT), :] = tok_ref[...][None]

    def quarter(place):
        return pl.ds(pl.multiple_of(place * PIECE, 16), PIECE)

    def og_spread(step, source):
        return remote(
            og.at[quarter(at_x(step)), :], og_rx.at[source], og_send.at[step], og_recv.at[source],
            dp=at_x(step),
        )

    nothing = jnp.zeros((PADDED - COLS, TOK), F32)
    og[COLS:, :] = nothing.astype(BF16)
    for index in range(NX):
        proj_own[index, COLS:, :] = nothing
        proj_tx[index, COLS:, :] = nothing.astype(BF16)
    og_copy.wait()
    og_rx[pl.ds(x, 1)] = og[quarter(x), :][None]
    for step in range(1, NX):
        start(og_spread(step, x))

    def turn(piece):
        columns = slice(piece * HALF // 2, (piece + 1) * HALF // 2)
        w_turned[columns, :] = jnp.transpose(w[:, columns])

    gain_copy.wait()
    gain_rows[...] = gain_ref[...].astype(F32)
    table = jnp.transpose(
        jnp.concatenate([gain_rows[pl.ds(12 * x, 12), :], jnp.zeros((116, 128), F32)], axis=0)
    )
    for i in range(12):
        gain[i * 128 : (i + 1) * 128, :] = jnp.broadcast_to(table[:, i : i + 1], (128, 128))

    for step in range(1, NZ):
        stat_z_copy(step, at_z(step)).wait_recv()
    stats = merge_stats(stat_z[...], float(FEAT))
    stat_y_tx[...] = stats
    stat_y[pl.ds(y, 1)] = stats[None]
    for step in range(1, NY):
        start(stat_y_copy(step, y))
    w_copy.wait()
    turn(0)
    turn(1)

    @pl.when(moves)
    def _():
        perm_copy().wait_recv()


    def gather_z(step, source):
        piece = z_block(y, source)
        return remote(piece, piece, zg_send.at[step], zg_recv.at[source], mp=mp(y, at_z(step)))

    def gather_y(way, step, k, source):
        piece = z_block(source, at_z(k))
        return remote(
            piece, piece, yg_send.at[way, step, k], yg_recv.at[way, step, k],
            mp=mp(at_y(1 - 2 * way), z),
        )

    for step in range(1, NZ):
        start(gather_z(step, z))
    for way in range(2):
        start(gather_y(way, 0, 0, y))
    turn(2)
    for step in range(1, NY):
        stat_y_copy(step, at_y(step)).wait_recv()
    stat_x[pl.ds(x, 1)] = merge_stats(stat_y[...], float(HALF))[None]
    for step in range(1, NX):
        start(stat_x_copy(step, x))
    turn(3)

    def receive(step, k):
        for way in range(2):
            if step < 4 or k % 2 == way:
                source = at_y(-step if way == 0 else step)
                gather_y(way, step - 1, k, source).wait_recv()
                if step < 3 or (step == 3 and k % 2 == way):
                    start(gather_y(way, step, k, source))

    arrivals = (0, 1, 3, 2)
    receive(1, 0)
    for k in arrivals[1:]:
        gather_z(k, at_z(k)).wait_recv()
        for way in range(2):
            start(gather_y(way, 0, k, y))
    def raw_copy(t):
        piece = pl.ds(0, FAR * CHUNK)
        return remote(
            rows.at[t, piece, :], site_rows.at[r, t // 2, piece, :],
            site_send.at[1 - r // 2, t], site_recv.at[r, t // 2],
            replica=2 * (1 - r // 2) + lax.rem(t, 2),
        )

    def site_stat_copy(source, to):
        return remote(
            stat_x, site_stat.at[source], site_stat_send.at[lax.rem(to, 2)], site_stat_recv.at[source], replica=to
        )

    def site_copy(source, t, replica, features):
        piece = pl.ds(0, features)
        return remote(
            normed.at[t, piece, :], site_rows.at[source, t // 2, piece, :],
            site_send.at[replica // 2, t], site_recv.at[source, t // 2], replica=replica,
        )

    def normalize(t):
        h = lax.rem(t, 2)
        statistics = stat_x[t // 2]
        scale = lax.rsqrt(statistics[1:2] * (1.0 / D) + 1e-06)
        column = gain[pl.ds(pl.multiple_of(h * HALF, HALF), HALF), :]
        value = (rows[t].astype(F32) - statistics[0:1]) * scale * column
        normed[pl.ds(t, 1)] = value.astype(BF16)[None]

        @pl.when(h != c)
        def _():
            site_copy(r, t, other_core, HALF).start()

    def project(step, low, high):
        group = completed(step)
        total = jnp.dot(
            w[low:high, :HALF], normed[2 * group], preferred_element_type=F32
        ) + jnp.dot(w[low:high, HALF:], normed[2 * group + 1], preferred_element_type=F32)
        proj_own[step - 1, low:high, :] = total
        proj_tx[step - 1, low:high, :] = total.astype(BF16)

    def proj_copy(step, other, source):
        return remote(
            proj_tx.at[step - 1, quarter(at_x(other)), :], proj_rx.at[step - 1, source],
            px_send.at[step - 1, other], px_recv.at[step - 1, source], dp=at_x(other),
        )

    def spread(step):
        for other in range(1, NX):
            start(proj_copy(step, other, x))

    def inner_x(step, other, source):
        piece = inner.at[r, completed(step), quarter(source), :]
        return remote(
            piece, piece, ix_send.at[step - 1, other], ix_recv.at[step - 1, source], dp=at_x(other)
        )

    def act_copy(step, source, to):
        return remote(
            act_tx.at[step - 1], act_all.at[quarter(source), :],
            act_send.at[step - 1], act_recv.at[source], dp=to,
        )

    def activate(step):
        group = completed(step)
        for other in range(1, NX):
            proj_copy(step, other, at_x(other)).wait_recv()
        projected = proj_own[step - 1, quarter(x), :]
        for other in range(1, NX):
            projected = projected + proj_rx[step - 1, at_x(other)].astype(F32)
        linear = lax.broadcasted_iota(jnp.int32, (PIECE, TOK), 0) + x * PIECE < QKV
        normal_cdf = 0.5 * (1.0 + lax.erf(projected * 0.7071067811865476))
        density = jnp.exp(-0.5 * projected * projected) * 0.3989422804014327
        slopes = jnp.where(linear, 1.0, normal_cdf + projected * density)
        inner[pl.ds(r, 1), pl.ds(group, 1), quarter(x), :] = (
            og_rx[group].astype(F32) * slopes
        ).astype(BF16)[None, None]
        for other in range(1, NX):
            start(inner_x(step, other, x))
        act_tx[step - 1] = jnp.where(linear, projected, projected * normal_cdf).astype(BF16)

        @pl.when(group != x)
        def _():
            act_copy(step, x, group).start()

        @pl.when(group == x)
        def _():
            act_all[quarter(x), :] = act_tx[step - 1]

    sign = 1 - 2 * b

    def completed(step):
        return at_y(step * sign if step % 2 else -step * sign) // 2

    def own_row():
        for step in range(1, NX):
            stat_x_copy(step, at_x(step)).wait_recv()
        normalize(y)
        for to in (other_lo, across):
            start(site_stat_copy(r, to))

    def tasks(step):
        yield lambda: normalize(at_y(step))
        if step < 4:
            yield lambda: normalize(at_y(-step))
        yield lambda: project(step, 0, COLS // 2)
        yield lambda: (project(step, COLS // 2, COLS), spread(step))
        if step == 2:
            yield wait_og
        if 1 < step < 4:
            yield lambda: activate(step - 1)

    def wait_og():
        for other in range(1, NX):
            og_spread(other, at_x(other)).wait_recv()

    start(raw_copy(y))
    receive(1, 1)
    own_row()
    receive(1, 3)
    receive(1, 2)
    for step in range(1, 5):
        start(raw_copy(at_y(step)))
        if step < 4:
            start(raw_copy(at_y(-step)))
        work = list(tasks(step))
        if step < 4:
            for k in arrivals:
                for task in work[:2]:
                    task()
                work = work[2:]
                receive(step + 1, k)
        for task in work:
            task()

    def inner_lo(replica, group):
        piece = inner.at[replica, group, pl.ds(0, COLS), :]
        return remote(
            piece, piece, lo_send.at[group], inner_recv.at[replica, group], replica=other_lo
        )

    def inner_core(replica, group):
        piece = inner.at[replica, group, pl.ds(0, COLS), :]
        return remote(
            piece, piece, core_send.at[replica // 2, group], inner_recv.at[replica, group],
            replica=other_core,
        )

    def take_group(step):
        group = completed(step)
        for other in range(1, NX):
            inner_x(step, other, at_x(other)).wait_recv()
        if step < 4:
            start(inner_lo(r, group))
        start(inner_core(r, group))
        part[:, pl.ds(pl.multiple_of(group * TOK, TOK), TOK)] = jnp.dot(
            w_turned[...], inner[r, group, 0:COLS, :], preferred_element_type=F32
        )

    def part_of(target, k):
        start_row = pl.multiple_of(lax.rem(target, 2) * HALF + at_z(k) * FEAT, FEAT)
        lane = pl.multiple_of(lax.rem(target // 2 + 2, NX) * TOK, TOK)
        return part[pl.ds(start_row, FEAT), pl.ds(lane, TOK)]

    def ring_copy(way, h, k):
        return remote(
            ytx.at[way, h - 1, k],
            yrx.at[way, h - 1, k],
            ys_send.at[way, h - 1, k],
            ys_recv.at[way, h - 1, k],
            mp=mp(at_y(1 - 2 * way), z),
        )

    def ring_send(way, h, k):
        value = part_of(at_y((1 - 2 * way) * h), k)
        if h < (4 if k % 2 == way else 3):
            ring_copy(way, h + 1, k).wait_recv()
            value = value + yrx[way, h, k].astype(F32)
        ytx[way, h - 1, k] = value.astype(BF16)
        start(ring_copy(way, h, k))

    def ring_round(h, ks):
        for k in ks:
            for way in range(2):
                if h < 4 or k % 2 == way:
                    ring_send(way, h, k)

    def wait_rows(replica, features):
        for g in range(NX):
            site_copy(replica, 2 * g, other_core, features).wait_recv()

    def weight_piece(left, right):
        return lax.dot_general(left, right, (((1,), (1,)), ((), ())), preferred_element_type=F32)

    def far_rows(replica):
        site_stat_copy(replica, other_lo).wait_recv()
        wait_rows(replica, FAR * CHUNK)
        column = gain[pl.ds(pl.multiple_of(c * HALF, HALF), FAR * CHUNK), :]
        for g in range(NX):
            statistics = site_stat[replica, g]
            scale = lax.rsqrt(statistics[1:2] * (1.0 / D) + 1e-06)
            value = (
                site_rows[replica, g, 0 : FAR * CHUNK, :].astype(F32) - statistics[0:1]
            ) * scale * column
            site_rows[pl.ds(replica, 1), g, 0 : FAR * CHUNK, :] = value.astype(BF16)[None]

    def add_near(step):
        g = completed(step)
        inner_core(other_core, g).wait_recv()
        left = jnp.concatenate([inner[r, g, 0:COLS, :], inner[other_core, g, 0:COLS, :]], axis=1)
        for k in reversed(range(PIECES)):
            piece = slice(k * CHUNK, (k + 1) * CHUNK)
            right = jnp.concatenate(
                [normed[2 * g + c, piece, :], site_rows[other_core, g, piece, :]], axis=1
            )
            w_sum[k] = weight_piece(left, right) + (w_sum[k] if step > 1 else 0.0)

    def far_piece(step, k):
        g = completed(step)
        left = jnp.concatenate([inner[other_lo, g, 0:COLS, :], inner[across, g, 0:COLS, :]], axis=1)
        piece = slice(k * CHUNK, (k + 1) * CHUNK)
        right = jnp.concatenate(
            [site_rows[other_lo, g, piece, :], site_rows[across, g, piece, :]], axis=1
        )
        return weight_piece(left, right) + (w_far[k] if step > 1 else 0.0)

    def add_far(step):
        inner_core(across, completed(step)).wait_recv()
        for k in range(FAR):
            w_far[k] = far_piece(step, k)

    def sum_copy():
        return remote(lo_tx, lo_rx, sum_send.at[0], sum_recv.at[0], replica=other_lo)

    def pass_on(step):
        inner_lo(other_lo, completed(step)).wait_recv()
        start(inner_core(other_lo, completed(step)))

    def done_copy(k, half):
        return remote(
            done.at[half, k], done.at[half, k], fin_send.at[k], fin_recv.at[k], replica=other_core
        )

    out_copies = []

    def out_copy(half, k, index):
        copy = pltpu.make_async_copy(
            done.at[half, k],
            wg_hbm.at[:, pl.ds(pl.multiple_of(half * HALF + k * CHUNK, CHUNK), CHUNK)],
            out_sem.at[index, k],
        )
        copy.start()
        out_copies.append(copy)

    order = (1, 3, 2, 0)
    take_group(1)
    ring_round(4, order)
    activate(3)
    take_group(2)
    ring_round(3, order)
    activate(4)
    take_group(3)
    ring_round(2, order)
    wait_rows(other_core, HALF)
    add_near(1)
    add_near(2)
    take_group(4)
    ring_round(1, order)
    def scatter_z(step, source):
        return remote(
            ztx.at[step], zrx.at[source], zs_send.at[step], zs_recv.at[source], mp=mp(y, at_z(step))
        )

    back_copy = remote(
        last_tx, ng_ref, perm_send.at[1], perm_recv.at[1], dp=back_x, mp=mp(y_back, z)
    )

    for k in order:
        for way in range(2):
            ring_copy(way, 1, k).wait_recv()
        total = part_of(y, k) + yrx[0, 0, k].astype(F32) + yrx[1, 0, k].astype(F32)
        if k:
            ztx[k] = total.astype(BF16)
            start(scatter_z(k, z))
    start(inner_lo(r, completed(4)))

    add_near(3)
    add_near(4)
    lo_tx[...] = w_sum[PIECES - 1].astype(BF16)
    start(sum_copy())
    pass_on(1)
    far_rows(other_lo)
    far_rows(across)
    pass_on(2)
    pass_on(3)
    for step in range(1, NZ):
        scatter_z(step, at_z(step)).wait_recv()
        total = total + zrx[at_z(step)].astype(F32)
    last_tx[...] = total.astype(BF16)
    start(back_copy)
    add_far(1)
    add_far(2)
    pass_on(4)
    add_far(3)

    def finish(k, total):
        done[pl.ds(c, 1), k] = (total * 0.25).astype(BF16)[None]
        start(done_copy(k, c))
        out_copy(c, k, 0)

    inner_core(across, completed(4)).wait_recv()
    for k in range(FAR):
        finish(k, w_sum[k] + far_piece(4, k))
    sum_copy().wait_recv()
    finish(PIECES - 1, lo_tx[...].astype(F32) + lo_rx[...].astype(F32))
    for k in range(PIECES):
        done_copy(k, 1 - c).wait_recv()
        out_copy(1 - c, k, 1)

    for other in range(1, NX):
        act_copy(1, at_x(other), at_x(other)).wait_recv()
    act_ref[...] = act_all[0:COLS, :]

    @pl.when(moves)
    def _():
        perm_copy().wait_send()


    for step in range(1, 5):
        @pl.when(completed(step) != x)
        def _(step=step):
            act_copy(step, x, completed(step)).wait_send()

    for g in range(NX):
        site_copy(r, 2 * g + 1 - c, other_core, HALF).wait_send()
    back_copy.wait_recv()
    for copy in copies:
        copy.wait_send()
    for copy in out_copies:
        copy.wait()


def hand_over(act_in, ng_in, wg_in, act_out, ng_out, wg_out, act, ng, wg, sem):
    pieces = [(act_in, act, act_out), (ng_in, ng, ng_out)]
    for i in range(6):
        piece = pl.ds(i * 112, 112)
        pieces.append((wg_in.at[piece, :], wg.at[piece, :], wg_out.at[piece, :]))
    loads = [
        pltpu.make_async_copy(source, held, sem.at[0, i]) for i, (source, held, _) in enumerate(pieces)
    ]
    stores = [
        pltpu.make_async_copy(held, target, sem.at[1, i]) for i, (_, held, target) in enumerate(pieces)
    ]
    for load in loads:
        load.start()
    for load, store in zip(loads, stores):
        load.wait()
        store.start()
    for store in stores:
        store.wait()


def local(tokens, norm_gain, joined_weight, output_grad):
    vmem = pl.BlockSpec(memory_space=pltpu.VMEM)
    anywhere = pl.BlockSpec(memory_space=pl.ANY)
    dma = pltpu.SemaphoreType.DMA
    scratch = [
        pltpu.VMEM((FEAT, TOK), BF16),
        pltpu.VMEM((D // 128, 128), BF16),
        pltpu.VMEM((COLS, 2 * HALF), BF16),
        pltpu.VMEM((2 * HALF, COLS), BF16),
        pltpu.VMEM((PADDED, TOK), BF16),
        pltpu.VMEM((NX, PIECE, TOK), BF16),
        pltpu.VMEM((D // 128, 128), F32),
        pltpu.VMEM((2 * HALF, TOK), F32),
        pltpu.VMEM((8, 128), F32),
        pltpu.VMEM((8, 128), F32),
        pltpu.VMEM((NZ, 8, 128), F32),
        pltpu.VMEM((NY, 8, 128), F32),
        pltpu.VMEM((NX, 8, 128), F32),
        pltpu.VMEM((4, NX, 8, 128), F32),
        pltpu.VMEM((NY, HALF, TOK), BF16),
        pltpu.VMEM((NY, HALF, TOK), BF16),
        pltpu.VMEM((4, NX, HALF, TOK), BF16),
        pltpu.VMEM((NX, PADDED, TOK), BF16),
        pltpu.VMEM((NX, NX, PIECE, TOK), BF16),
        pltpu.VMEM((NX, PADDED, TOK), F32),
        pltpu.VMEM((NX, PIECE, TOK), BF16),
        pltpu.VMEM((PADDED, TOK), BF16),
        pltpu.VMEM((4, NX, PADDED, TOK), BF16),
        pltpu.VMEM((2 * HALF, NX * TOK), F32),
        pltpu.VMEM((2, 4, NZ, FEAT, TOK), BF16),
        pltpu.VMEM((2, 4, NZ, FEAT, TOK), BF16),
        pltpu.VMEM((NZ, FEAT, TOK), BF16),
        pltpu.VMEM((NZ, FEAT, TOK), BF16),
        pltpu.VMEM((FEAT, TOK), BF16),
        pltpu.VMEM((PIECES, COLS, CHUNK), F32),
        pltpu.VMEM((FAR, COLS, CHUNK), F32),
        pltpu.VMEM((COLS, CHUNK), BF16),
        pltpu.VMEM((COLS, CHUNK), BF16),
        pltpu.VMEM((2, PIECES, COLS, CHUNK), BF16),
        dma((4,)),
        dma((2, PIECES)),
        dma((NZ + NY + NX,)),
        dma((NZ + NY + NX,)),
        dma((2,)),
        dma((2,)),
        dma((NZ,)),
        dma((NZ,)),
        dma((2, 4, NZ)),
        dma((2, 4, NZ)),
        dma((2, NY)),
        dma((4, NX)),
        dma((2,)),
        dma((4,)),
        dma((NX,)),
        dma((NX,)),
        dma((NX, NX)),
        dma((NX, NX)),
        dma((NX, NX)),
        dma((NX, NX)),
        dma((NX,)),
        dma((NX,)),
        dma((NX,)),
        dma((2, NX)),
        dma((4, NX)),
        dma((2, 4, NZ)),
        dma((2, 4, NZ)),
        dma((NZ,)),
        dma((NZ,)),
        dma((1,)),
        dma((1,)),
        dma((PIECES,)),
        dma((PIECES,)),
    ]
    shapes = (
        jax.ShapeDtypeStruct((COLS, TOK), BF16),
        jax.ShapeDtypeStruct((FEAT, TOK), BF16),
        jax.ShapeDtypeStruct((COLS, 2 * HALF), BF16),
    )
    results = pl.pallas_call(
        kernel,
        out_shape=shapes,
        in_specs=[anywhere] * 4,
        out_specs=(vmem, vmem, anywhere),
        scratch_shapes=scratch,
        compiler_params=pltpu.CompilerParams(
            collective_id=0, has_side_effects=True, vmem_limit_bytes=56 * 1024 * 1024
        ),
        cost_estimate=pl.CostEstimate(flops=3200000000, bytes_accessed=5000000, transcendentals=200000),
    )(
        tokens.T,
        norm_gain.reshape(D // 128, 128),
        output_grad.T,
        joined_weight.T,
    )
    activated, normed_grad, weight_grad = pl.pallas_call(
        hand_over,
        out_shape=shapes,
        in_specs=[anywhere] * 3,
        out_specs=(anywhere,) * 3,
        scratch_shapes=[pltpu.VMEM(shape.shape, BF16) for shape in shapes] + [dma((2, 8))],
        cost_estimate=pl.CostEstimate(flops=0, bytes_accessed=4600000, transcendentals=0),
    )(*results)
    return activated.T, normed_grad.T, weight_grad.T


def solution(mesh):
    in_specs = (P(("replica", "dp"), "mp"), P(), P("dp", "mp"), P(("replica", "dp"), "mp"))
    out_specs = (P(("replica", "dp"), "mp"), P(("replica", "dp"), "mp"), P("dp", "mp"))
    return jax.shard_map(local, mesh=mesh, in_specs=in_specs, out_specs=out_specs, check_vma=False)
```
